32 devices in a mesh: vol: 16 (over z, y, x), src: 2 (over core).
Axes of the slice: x: 2, y: 2, z: 4, core: 2. Of those that a mesh axis runs over, the one named last changes fastest.
Arguments:
- excitation: float32 [32, 32, 32, 128], P(None, 'vol', 'src'), may hold values from -6 to 6
- start: float32 [32, 32, 32, 128], P(None, 'vol', 'src'), may hold values from -4 to 4
- material: int32 [32, 32, 128], P('vol', 'src'), may hold values from 0 to 2
- face_cell: int32 [16, 2, 64], P('vol', 'src'), may hold values from 0 to 4095
- face_count: int32 [16, 2, 16], P('vol', 'src'), may hold values from 0 to 4, as said below
- face_weight: float32 [16, 2, 64], P('vol', 'src'), may hold values from 0.5 to 1.5
- slot_panel: int32 [16, 2, 64], P('vol', 'src'), may hold values from 0 to 2047
- target_points: float32 [3, 65536], P(None, 'vol'), may hold values from 0 to 1
- source_points: float32 [3, 65536], P(None, 'src'), may hold values from 0 to 1
Outputs:
- potential: float32 [32, 32, 32, 128], P(None, 'vol', 'src')
- flux: float32 [32, 65536], P(None, ('vol', 'src'))
The draws below stay inside these ranges and needn't reach their ends.
Inputs may be any that keep to these rules, and one draw needn't show every extreme that they name: A device has at most 4 live slots for one owner (the first face_count ones); in every draw some owner receives 4 live faces from every device.
All inputs are finite; a program needn't handle non-finite values.
Results may differ from the reference program's by a relative error of at most 0.0023.
The reference program's roundings to bfloat16 on the way (of `density` and `kernel`) count: a program that leaves them out, or rounds other values in their place, can miss the bound.
Values may be sent and summed in bfloat16 or wider, within the bound.
A program may use at most 64 MiB of HBM per device.

```python
import jax
import jax.numpy as jnp
from jax import lax

EXC = 32
CX = 2
CY = 16
CZ = 128
P_SIZE = 65536
CAP = 4
ITERS = 2
SWEEPS = 2
NX = 32
NY = 32
NZ = 128
CELLS = 4096
PIECE = 2048
N_VOL = 16
N_SRC = 2


def draw_face_count(key, part):
    limit_key = jax.random.fold_in(key, 11)
    spread_key = jax.random.fold_in(key, 12)
    full_key = jax.random.fold_in(key, 13)
    limit = jax.random.randint(limit_key, (N_VOL, N_SRC, 1), 1, CAP + 1)
    lowest = limit // 2
    raw_draw = jax.random.randint(spread_key, (N_VOL, N_SRC, N_VOL), 0, 1048576)
    counts = lowest + raw_draw % (limit - lowest + 1)
    full_owner = jax.random.randint(full_key, (), 0, N_VOL)
    owner_ids = jnp.arange(N_VOL, dtype=jnp.int32)[None, None, :]
    return jnp.where(owner_ids == full_owner, CAP, counts).astype(jnp.int32)


def touch_ends(values, stream_key, least, largest):
    longest = values.shape.index(max(values.shape))
    spots = []
    for shift in (0, 1):
        where = [jax.random.randint(jax.random.fold_in(stream_key, axis), (), 0, length) for axis, length in enumerate(values.shape)]
        where[longest] = (where[longest] + shift) % values.shape[longest]
        spots.append(tuple(where))
    return values.at[spots[0]].set(least).at[spots[1]].set(largest)


def block_levels(key, dims, cuts, least, largest):
    def one(position, blocks):
        draws = jax.random.uniform(jax.random.fold_in(jax.random.fold_in(key, 6), position), (blocks,), jnp.float32, least / len(cuts), largest / len(cuts))
        return jnp.repeat(jnp.exp(draws), dims[position] // blocks).reshape((-1,) + (1,) * (len(dims) - position - 1))

    level = one(*cuts[0])
    for cut in cuts[1:]:
        level = level * one(*cut)
    return level


def normal_values(stream_key, extent, deviation, bound, cuts=(), held_as=jnp.bfloat16):
    gain = block_levels(stream_key, extent, cuts, -0.22, 0.18) if cuts else 1.0
    array = jax.random.normal(stream_key, extent, jnp.float32) * deviation * gain
    return jnp.minimum(jnp.maximum(array, -bound), bound).astype(held_as)


def setup_inputs(seed: int = 0) -> dict:
    seeds = jax.random.split(jax.random.key(seed), 10)
    excitation = normal_values(seeds[0], (EXC, NX, NY, NZ), 1.0, 6.0, ((1, 16), (2, 2)), jnp.float32)
    start = normal_values(seeds[1], (EXC, NX, NY, NZ), 0.5, 4.0, ((1, 16), (2, 2)), jnp.float32)
    material = touch_ends(jax.random.randint(seeds[2], (NX, NY, NZ), 0, 3), jax.random.fold_in(seeds[2], 1), 0, 2).astype(jnp.int32)
    face_cell = touch_ends(jax.random.randint(seeds[3], (N_VOL, N_SRC, N_VOL * CAP), 0, CELLS), jax.random.fold_in(seeds[3], 1), 0, CELLS - 1).astype(jnp.int32)
    face_count = draw_face_count(jax.random.fold_in(seeds[9], 71), 0)
    face_weight = jnp.clip(0.5 + 1.0 * jax.random.uniform(seeds[5], (N_VOL, N_SRC, N_VOL * CAP), jnp.float32) ** block_levels(seeds[5], (N_VOL, N_SRC, N_VOL * CAP), ((0, 16), (1, 2)), -0.2, 0.2), 0.5, 1.5)
    slot_panel = touch_ends(jax.random.randint(seeds[6], (N_VOL, N_SRC, N_VOL * CAP), 0, PIECE), jax.random.fold_in(seeds[6], 1), 0, PIECE - 1).astype(jnp.int32)
    target_points = jnp.clip(1.0 * jax.random.uniform(seeds[7], (3, P_SIZE), jnp.float32) ** block_levels(seeds[7], (3, P_SIZE), ((1, 16),), -0.2, 0.2), 0.0, 1.0)
    source_points = jnp.clip(1.0 * jax.random.uniform(seeds[8], (3, P_SIZE), jnp.float32) ** block_levels(seeds[8], (3, P_SIZE), ((1, 2),), -0.2, 0.2), 0.0, 1.0)
    return {"excitation": excitation, "start": start, "material": material, "face_cell": face_cell, "face_count": face_count, "face_weight": face_weight, "slot_panel": slot_panel, "target_points": target_points, "source_points": source_points}


NU_BASE = (1.0, 0.05, 0.4)
NU_SATURATION = (0.0, 0.9, 0.3)
RELAXATION = 0.8
SOFTENING = 0.05

def reluctivity(grad_sq, material):
    base_value = jnp.zeros(material.shape, jnp.float32)
    slope_value = jnp.zeros(material.shape, jnp.float32)
    for material_id in range(3):
        picked = material == material_id
        base_value = jnp.where(picked, NU_BASE[material_id], base_value)
        slope_value = jnp.where(picked, NU_SATURATION[material_id], slope_value)
    return base_value[None] + slope_value[None] * grad_sq / (1.0 + grad_sq)

def gradient_sq(padded):
    along_x = 0.5 * (padded[:, 2:, 1:-1, 1:-1] - padded[:, :-2, 1:-1, 1:-1])
    along_y = 0.5 * (padded[:, 1:-1, 2:, 1:-1] - padded[:, 1:-1, :-2, 1:-1])
    along_z = 0.5 * (padded[:, 1:-1, 1:-1, 2:] - padded[:, 1:-1, 1:-1, :-2])
    return along_x * along_x + along_y * along_y + along_z * along_z

def relax(padded, weights, diagonal, forcing):
    center = padded[:, 1:-1, 1:-1, 1:-1]
    neighbours = (padded[:, 2:, 1:-1, 1:-1], padded[:, :-2, 1:-1, 1:-1], padded[:, 1:-1, 2:, 1:-1], padded[:, 1:-1, :-2, 1:-1], padded[:, 1:-1, 1:-1, 2:], padded[:, 1:-1, 1:-1, :-2])
    applied = diagonal * center
    for weight, neighbour in zip(weights, neighbours):
        applied = applied - weight * neighbour
    return center + RELAXATION * (forcing - applied) / diagonal

def panel_flux(density_src, target_points, source_points):
    block_len = 512
    target_blocks = target_points.reshape(3, P_SIZE // block_len, block_len).transpose(1, 0, 2)

    def one_block(block_points):
        dist_sq = jnp.zeros((block_len, P_SIZE), jnp.float32)
        for component in range(3):
            offset = block_points[component][:, None] - source_points[component][None, :]
            dist_sq = dist_sq + offset * offset
        kernel = lax.rsqrt(dist_sq + SOFTENING * SOFTENING).astype(jnp.bfloat16)
        return jnp.dot(density_src, kernel.T, preferred_element_type=jnp.float32)
    flux_blocks = lax.map(one_block, target_blocks)
    return flux_blocks.transpose(1, 0, 2).reshape(EXC, P_SIZE)

def reference(excitation, start, material, face_cell, face_count, face_weight, slot_panel, target_points, source_points):
    vol_ids = jnp.arange(N_VOL, dtype=jnp.int32)[:, None, None]
    src_ids = jnp.arange(N_SRC, dtype=jnp.int32)[None, :, None]
    slot_ids = jnp.arange(N_VOL * CAP, dtype=jnp.int32)[None, None, :]
    owner_ids = slot_ids // CAP
    rank_ids = slot_ids % CAP
    local_x = face_cell // (CY * CZ)
    local_y = face_cell // CZ % CY
    local_z = face_cell % CZ
    cell_index = (((vol_ids * CX + local_x) * NY + src_ids * CY + local_y) * NZ + local_z).reshape(-1).astype(jnp.int32)
    live_count = jnp.take_along_axis(face_count, jnp.broadcast_to(owner_ids, face_cell.shape), axis=2)
    slot_scale = jnp.where(rank_ids < live_count, face_weight, 0.0).reshape(-1)
    panel_local = slot_panel[owner_ids, src_ids, vol_ids * CAP + rank_ids]
    panel_index = ((owner_ids * N_SRC + src_ids) * PIECE + panel_local).reshape(-1).astype(jnp.int32)
    potential = start
    flux = jnp.zeros((EXC, P_SIZE), jnp.float32)
    for outer_index in range(ITERS):
        padded = jnp.pad(potential, ((0, 0), (1, 1), (1, 1), (1, 1)))
        nu_cells = reluctivity(gradient_sq(padded), material)
        nu_pad = jnp.pad(nu_cells, ((0, 0), (1, 1), (1, 1), (1, 1)), mode='edge')
        weights = (0.5 * (nu_cells + nu_pad[:, 2:, 1:-1, 1:-1]), 0.5 * (nu_cells + nu_pad[:, :-2, 1:-1, 1:-1]), 0.5 * (nu_cells + nu_pad[:, 1:-1, 2:, 1:-1]), 0.5 * (nu_cells + nu_pad[:, 1:-1, :-2, 1:-1]), 0.5 * (nu_cells + nu_pad[:, 1:-1, 1:-1, 2:]), 0.5 * (nu_cells + nu_pad[:, 1:-1, 1:-1, :-2]))
        diagonal = weights[0] + weights[1] + weights[2] + weights[3] + weights[4] + weights[5]
        flat_potential = potential.reshape(EXC, -1)
        traces = flat_potential[:, cell_index] * slot_scale[None, :]
        density = jnp.zeros((EXC, P_SIZE), jnp.float32).at[:, panel_index].add(traces).astype(jnp.bfloat16)
        density_src = density.reshape(EXC, N_VOL, N_SRC, PIECE).transpose(0, 2, 1, 3).reshape(EXC, P_SIZE)
        flux = panel_flux(density_src, target_points, source_points) * float(P_SIZE) ** (-0.5)
        surface = jnp.zeros((EXC, NX * NY * NZ), jnp.float32).at[:, cell_index].add(flux[:, panel_index] * slot_scale[None, :])
        forcing = excitation + surface.reshape(excitation.shape)
        for sweep_index in range(SWEEPS):
            potential = relax(jnp.pad(potential, ((0, 0), (1, 1), (1, 1), (1, 1))), weights, diagonal, forcing)
    return (potential, flux)
```

```python
import jax
import jax.numpy as jnp
from jax import lax
from jax.sharding import PartitionSpec as P

P_SIZE = 65536
ITERS = 2
SWEEPS = 2


NU_BASE = (1.0, 0.05, 0.4)
NU_SATURATION = (0.0, 0.9, 0.3)
RELAXATION = 0.8
SOFTENING = 0.05


def extended(block, sides, width):
    for axis, dim in sides:
        count = lax.axis_size(axis)
        forward = [(i, i + 1) for i in range(count - 1)]
        backward = [(target, source) for source, target in forward]
        low = lax.ppermute(
            lax.slice_in_dim(block, block.shape[dim] - width, None, axis=dim), axis, forward
        )
        high = lax.ppermute(lax.slice_in_dim(block, 0, width, axis=dim), axis, backward)
        block = jnp.concatenate([low, block, high], axis=dim)
    return block


def reluctivity(grad_sq, material):
    base_value = jnp.zeros(material.shape, jnp.float32)
    slope_value = jnp.zeros(material.shape, jnp.float32)
    for material_id in range(3):
        picked = material == material_id
        base_value = jnp.where(picked, NU_BASE[material_id], base_value)
        slope_value = jnp.where(picked, NU_SATURATION[material_id], slope_value)
    return base_value[None] + slope_value[None] * grad_sq / (1.0 + grad_sq)


def gradient_sq(padded):
    along_x = 0.5 * (padded[:, 2:, 1:-1, 1:-1] - padded[:, :-2, 1:-1, 1:-1])
    along_y = 0.5 * (padded[:, 1:-1, 2:, 1:-1] - padded[:, 1:-1, :-2, 1:-1])
    along_z = 0.5 * (padded[:, 1:-1, 1:-1, 2:] - padded[:, 1:-1, 1:-1, :-2])
    return along_x * along_x + along_y * along_y + along_z * along_z


def pad_depth(values):
    return jnp.pad(values, ((0, 0), (0, 0), (0, 0), (1, 1)))


def face_weights(nu_ext, domain_edges):
    first_x, last_x, first_y, last_y = domain_edges
    interior = nu_ext[:, 1:-1, 1:-1]
    low_x = jnp.where(first_x, interior[:, :1], nu_ext[:, :1, 1:-1])
    high_x = jnp.where(last_x, interior[:, -1:], nu_ext[:, -1:, 1:-1])
    column = jnp.concatenate([low_x, interior, high_x], axis=1)
    low_y = jnp.where(first_y, interior[:, :, :1], nu_ext[:, 1:-1, :1])
    high_y = jnp.where(last_y, interior[:, :, -1:], nu_ext[:, 1:-1, -1:])
    row_ext = jnp.concatenate([low_y, interior, high_y], axis=2)
    depth_ext = jnp.pad(interior, ((0, 0), (0, 0), (0, 0), (1, 1)), mode="edge")
    return (
        0.5 * (interior + column[:, 2:]),
        0.5 * (interior + column[:, :-2]),
        0.5 * (interior + row_ext[:, :, 2:]),
        0.5 * (interior + row_ext[:, :, :-2]),
        0.5 * (interior + depth_ext[:, :, :, 2:]),
        0.5 * (interior + depth_ext[:, :, :, :-2]),
    )


def relax(padded, weights, diagonal, forcing):
    center = padded[:, 1:-1, 1:-1, 1:-1]
    neighbours = (
        padded[:, 2:, 1:-1, 1:-1],
        padded[:, :-2, 1:-1, 1:-1],
        padded[:, 1:-1, 2:, 1:-1],
        padded[:, 1:-1, :-2, 1:-1],
        padded[:, 1:-1, 1:-1, 2:],
        padded[:, 1:-1, 1:-1, :-2],
    )
    applied = diagonal * center
    for weight, neighbour in zip(weights, neighbours):
        applied = applied - weight * neighbour
    return center + RELAXATION * (forcing - applied) / diagonal


def kernel_block(targets, places):
    dist_sq = jnp.zeros((targets.shape[1], places.shape[1]), jnp.float32)
    for component in range(3):
        offset = targets[component][:, None] - places[component][None, :]
        dist_sq = dist_sq + offset * offset
    return lax.rsqrt(dist_sq + SOFTENING * SOFTENING).astype(jnp.bfloat16)


def with_rim(potential):
    return extended(potential, (("vol", 1), ("src", 2)), 1)


def per_device(
    excitation,
    start,
    material,
    face_cell,
    face_count,
    face_weight,
    slot_panel,
    target_points,
    source_points,
):
    vol_count = lax.axis_size("vol")
    first_x = lax.axis_index("vol") == 0
    last_x = lax.axis_index("vol") == vol_count - 1
    first_y = lax.axis_index("src") == 0
    last_y = lax.axis_index("src") == lax.axis_size("src") - 1
    domain_edges = (first_x, last_x, first_y, last_y)
    exc_count, width_x, width_y, depth_len = excitation.shape
    cell_count = width_x * width_y * depth_len
    slot_cells = face_cell.reshape(-1)
    slot_count = slot_cells.shape[0]
    capacity = slot_count // vol_count
    piece_len = source_points.shape[1] // vol_count
    target_len = target_points.shape[1]
    slot_rank = jnp.arange(slot_count, dtype=jnp.int32) % capacity
    live_count = jnp.repeat(face_count.reshape(-1), capacity, total_repeat_length=slot_count)
    slot_scale = jnp.where(slot_rank < live_count, face_weight.reshape(-1), 0.0)
    compact = slot_count < piece_len
    vol_index = lax.axis_index("vol")
    src_index = lax.axis_index("src")
    src_count = lax.axis_size("src")
    panels = slot_panel.reshape(-1)
    if compact:
        own_points = jnp.concatenate(
            [
                jnp.take(lax.dynamic_slice_in_dim(source_points, vol_index * piece_len, piece_len, 1), panels, axis=1),
                jnp.take(lax.dynamic_slice_in_dim(target_points, src_index * piece_len, piece_len, 1), panels, axis=1),
                panels.astype(jnp.float32)[None],
            ]
        )
        own_targets = lax.dynamic_slice_in_dim(target_points, src_index * piece_len, piece_len, 1)
    else:
        owner_table = (
            panels[:, None] == jnp.arange(piece_len, dtype=jnp.int32)[None, :]
        ).astype(jnp.float32)
    flux_scale = float(P_SIZE) ** (-0.5)
    potential = start
    flux_own = jnp.zeros((exc_count, piece_len), jnp.float32)
    for outer_index in range(ITERS):
        current = with_rim(potential)
        nu_own = reluctivity(gradient_sq(pad_depth(current)), material)
        nu_ext = extended(nu_own, (("vol", 1), ("src", 2)), 1)
        weights = face_weights(nu_ext, domain_edges)
        diagonal = weights[0] + weights[1] + weights[2] + weights[3] + weights[4] + weights[5]
        cell_values = jnp.take(potential.reshape(exc_count, cell_count), slot_cells, axis=1)
        if compact:
            traces = (cell_values * slot_scale[None, :]).T
            message = traces if outer_index else jnp.concatenate([traces, own_points.T], axis=1)
            gathered = lax.all_gather(message, ("vol", "src"), axis=0, tiled=False)
            gathered = gathered.reshape(vol_count, src_count, slot_count, -1)
            if outer_index == 0:
                points = gathered[..., exc_count:]
                places = points[..., :3].reshape(-1, 3).T
                ids = points[..., 6]
                same = ids[..., :, None] == ids[..., None, :]
                rank = jnp.arange(slot_count)
                earlier = same & (rank[None, :] < rank[:, None])
                merge = (same & ~jnp.any(earlier, axis=-1)[..., None]).astype(jnp.float32)
                mine = lax.dynamic_index_in_dim(points, src_index, 1, keepdims=False)
                mine = mine.reshape(vol_count, vol_count, capacity, -1)
                mine = lax.dynamic_index_in_dim(mine, vol_index, 1, keepdims=False)
                slot_targets = mine[..., 3:6].reshape(-1, 3).T
                slot_kernel = kernel_block(slot_targets, places)
            arrived = gathered[..., :exc_count].reshape(
                vol_count, src_count, vol_count, capacity, exc_count
            )
            arrived = arrived.transpose(2, 1, 0, 3, 4).reshape(
                vol_count, src_count, slot_count, exc_count
            )
            density = jnp.einsum(
                "wsij,wsje->wsie", merge, arrived, precision=lax.Precision.HIGHEST
            )
            density = density.reshape(-1, exc_count).astype(jnp.bfloat16)
            returned = flux_scale * jnp.einsum(
                "tn,ne->te", slot_kernel, density, preferred_element_type=jnp.float32
            )
            if outer_index == ITERS - 1:
                flux_own = flux_scale * jnp.einsum(
                    "ne,tn->et",
                    density,
                    kernel_block(own_targets, places),
                    preferred_element_type=jnp.float32,
                )
        else:
            outgoing = (cell_values * slot_scale[None, :]).T.reshape(vol_count, capacity * exc_count)
            arrived = lax.all_to_all(outgoing, "vol", split_axis=0, concat_axis=0, tiled=True).reshape(
                slot_count, exc_count
            )
            density = jnp.dot(
                arrived.T,
                owner_table,
                precision=lax.Precision.HIGHEST,
                preferred_element_type=jnp.float32,
            ).astype(jnp.bfloat16)
            block_piece = lax.all_gather(density, "vol", axis=1, tiled=True)
            piece_count = block_piece.shape[1]
            step_len = 1024

            def one_step(step_index, partial_value):
                offset_index = step_index * step_len
                segment = lax.dynamic_slice_in_dim(block_piece, offset_index, step_len, 1)
                places = lax.dynamic_slice_in_dim(source_points, offset_index, step_len, 1)
                dist_sq = jnp.zeros((target_len, step_len), jnp.float32)
                for component in range(3):
                    offset = target_points[component][:, None] - places[component][None, :]
                    dist_sq = dist_sq + offset * offset
                kernel = lax.rsqrt(dist_sq + SOFTENING * SOFTENING).astype(jnp.bfloat16)
                return partial_value + jnp.einsum(
                    "en,tn->et", segment, kernel, preferred_element_type=jnp.float32
                )

            partial_flux = lax.fori_loop(
                0, piece_count // step_len, one_step, jnp.zeros((exc_count, target_len), jnp.float32)
            )
            flux_sum = lax.psum_scatter(partial_flux, "src", scatter_dimension=1, tiled=True)
            flux_own = flux_sum * flux_scale
            per_slot = jnp.dot(
                flux_own,
                owner_table.T,
                precision=lax.Precision.HIGHEST,
                preferred_element_type=jnp.float32,
            )
            returned = lax.all_to_all(
                per_slot.T.reshape(vol_count, capacity * exc_count),
                "vol",
                split_axis=0,
                concat_axis=0,
                tiled=True,
            ).reshape(slot_count, exc_count)
        contribution = returned.T * slot_scale[None, :]
        surface = (
            jnp.zeros((exc_count, cell_count), jnp.float32).at[:, slot_cells].add(contribution)
        )
        forcing = excitation + surface.reshape(excitation.shape)
        for sweep_index in range(SWEEPS):
            if sweep_index > 0:
                current = with_rim(potential)
            potential = relax(pad_depth(current), weights, diagonal, forcing)
    return (potential, flux_own)


def solution(mesh):
    return jax.shard_map(
        per_device,
        mesh=mesh,
        in_specs=(
            P(None, "vol", "src", None),
            P(None, "vol", "src", None),
            P("vol", "src", None),
            P("vol", "src", None),
            P("vol", "src", None),
            P("vol", "src", None),
            P("vol", "src", None),
            P(None, "vol"),
            P(None, "src"),
        ),
        out_specs=(P(None, "vol", "src", None), P(None, ("vol", "src"))),
        check_vma=False,
    )
```

```python
import functools

import jax
import jax.numpy as jnp
from jax import lax
from jax.experimental import pallas as pl
from jax.experimental.pallas import tpu as pltpu
from jax.sharding import PartitionSpec as P

P_SIZE = 65536
ITERS = 2
SWEEPS = 2


NU_BASE = (1.0, 0.05, 0.4)
NU_SATURATION = (0.0, 0.9, 0.3)
RELAXATION = 0.8
SOFTENING = 0.05


def extended(block, sides, width):
    for axis, dim in sides:
        count = lax.axis_size(axis)
        forward = [(i, i + 1) for i in range(count - 1)]
        backward = [(target, source) for source, target in forward]
        low = lax.ppermute(
            lax.slice_in_dim(block, block.shape[dim] - width, None, axis=dim), axis, forward
        )
        high = lax.ppermute(lax.slice_in_dim(block, 0, width, axis=dim), axis, backward)
        block = jnp.concatenate([low, block, high], axis=dim)
    return block


def reluctivity(grad_sq, material):
    base_value = jnp.zeros(material.shape, jnp.float32)
    slope_value = jnp.zeros(material.shape, jnp.float32)
    for material_id in range(3):
        picked = material == material_id
        base_value = jnp.where(picked, NU_BASE[material_id], base_value)
        slope_value = jnp.where(picked, NU_SATURATION[material_id], slope_value)
    return base_value[None] + slope_value[None] * grad_sq / (1.0 + grad_sq)


def gradient_sq(padded):
    along_x = 0.5 * (padded[:, 2:, 1:-1, 1:-1] - padded[:, :-2, 1:-1, 1:-1])
    along_y = 0.5 * (padded[:, 1:-1, 2:, 1:-1] - padded[:, 1:-1, :-2, 1:-1])
    along_z = 0.5 * (padded[:, 1:-1, 1:-1, 2:] - padded[:, 1:-1, 1:-1, :-2])
    return along_x * along_x + along_y * along_y + along_z * along_z


def pad_depth(values):
    return jnp.pad(values, ((0, 0), (0, 0), (0, 0), (1, 1)))


def face_weights(nu_ext, domain_edges):
    first_x, last_x, first_y, last_y = domain_edges
    interior = nu_ext[:, 1:-1, 1:-1]
    low_x = jnp.where(first_x, interior[:, :1], nu_ext[:, :1, 1:-1])
    high_x = jnp.where(last_x, interior[:, -1:], nu_ext[:, -1:, 1:-1])
    column = jnp.concatenate([low_x, interior, high_x], axis=1)
    low_y = jnp.where(first_y, interior[:, :, :1], nu_ext[:, 1:-1, :1])
    high_y = jnp.where(last_y, interior[:, :, -1:], nu_ext[:, 1:-1, -1:])
    row_ext = jnp.concatenate([low_y, interior, high_y], axis=2)
    depth_ext = jnp.pad(interior, ((0, 0), (0, 0), (0, 0), (1, 1)), mode="edge")
    return (
        0.5 * (interior + column[:, 2:]),
        0.5 * (interior + column[:, :-2]),
        0.5 * (interior + row_ext[:, :, 2:]),
        0.5 * (interior + row_ext[:, :, :-2]),
        0.5 * (interior + depth_ext[:, :, :, 2:]),
        0.5 * (interior + depth_ext[:, :, :, :-2]),
    )


def relax(padded, weights, diagonal, forcing):
    center = padded[:, 1:-1, 1:-1, 1:-1]
    neighbours = (
        padded[:, 2:, 1:-1, 1:-1],
        padded[:, :-2, 1:-1, 1:-1],
        padded[:, 1:-1, 2:, 1:-1],
        padded[:, 1:-1, :-2, 1:-1],
        padded[:, 1:-1, 1:-1, 2:],
        padded[:, 1:-1, 1:-1, :-2],
    )
    applied = diagonal * center
    for weight, neighbour in zip(weights, neighbours):
        applied = applied - weight * neighbour
    return center + RELAXATION * (forcing - applied) / diagonal


def kernel_block(targets, places):
    dist_sq = jnp.zeros((targets.shape[1], places.shape[1]), jnp.float32)
    for component in range(3):
        offset = targets[component][:, None] - places[component][None, :]
        dist_sq = dist_sq + offset * offset
    return lax.rsqrt(dist_sq + SOFTENING * SOFTENING).astype(jnp.bfloat16)


def with_rim(potential):
    return extended(potential, (("vol", 1), ("src", 2)), 1)


MESH = pl.DeviceIdType.MESH
LANES = 128
TILE = 8
NT = (((1,), (1,)), ((), ()))
NN = (((1,), (0,)), ((), ()))


def split_dot(values, selector, dims):
    total = None
    for _ in range(3):
        part = values.astype(jnp.bfloat16)
        term = lax.dot_general(part, selector, dims, preferred_element_type=jnp.float32)
        total = term if total is None else total + term
        values = values - part.astype(jnp.float32)
    return total


def pair_kernel(columns, rows):
    dist_sq = None
    for column, row in zip(columns, rows):
        offset = column - row
        dist_sq = offset * offset if dist_sq is None else dist_sq + offset * offset
    return lax.rsqrt(dist_sq + SOFTENING * SOFTENING).astype(jnp.bfloat16)


def fused_kernel(
    vol_count, src_count, capacity, flux_scale,
    start_ref, exc_ref, mat_ref, cell_ref, scale_ref, geo_ref, merge_ref, target_ref,
    out_ref, flux_ref,
    pe, pf, nu, forcing, a_send, ax, ay, ac, b_send, bx, by, mat_near,
    tr_send, tr_recv, de_send, de_recv, ge_recv, ge_all, slot_kernel, dens_all,
    halo_ss, halo_rs, tr_ss, tr_rs, de_ss, de_rs, ge_ss, ge_rs,
):
    width_x, width_y, exc_count, depth = start_ref.shape
    count = vol_count * src_count
    v, s = lax.axis_index("vol"), lax.axis_index("src")
    me = v * src_count + s
    group = TILE // capacity
    slot_count = vol_count * capacity
    first_x, last_x = v == 0, v == vol_count - 1
    first_y, last_y = s == 0, s == src_count - 1

    def device(index):
        return (index // src_count, lax.rem(index, src_count))

    barrier = pltpu.get_barrier_semaphore()

    def greet(step, carry):
        other = lax.rem(me + step, count)
        pl.semaphore_signal(barrier, inc=1, device_id=device(other), device_id_type=MESH)
        return carry

    lax.fori_loop(1, count, greet, 0)

    lane = lax.broadcasted_iota(jnp.int32, (exc_count, depth), 1)
    at_low, at_high = lane == 0, lane == depth - 1
    cell_row = cell_ref[0:1, :]
    cell_depth = cell_ref[1:2, :]
    slot_scale = scale_ref[0:1, :]
    pick_depth = (
        lax.broadcasted_iota(jnp.int32, (depth, LANES), 0) == cell_depth
    ).astype(jnp.float32).astype(jnp.bfloat16)
    chunk = 8

    def traces_of(read):
        total = jnp.zeros((exc_count, LANES), jnp.float32)
        for x in range(width_x):
            for y0 in range(0, width_y, chunk):
                block = read(x, y0).reshape(chunk * exc_count, depth)
                taken = split_dot(block, pick_depth, NN)
                for k in range(chunk):
                    row = x * width_y + y0 + k
                    total = total + jnp.where(
                        cell_row == row, taken[k * exc_count : (k + 1) * exc_count], 0.0
                    )
        total = total * slot_scale
        return jnp.concatenate([total] * (LANES // exc_count), axis=0).T

    def each_near(direction):
        dv, ds = direction
        sends, gets = True, True
        if dv > 0:
            sends, gets = jnp.logical_not(last_x), jnp.logical_not(first_x)
        elif dv < 0:
            sends, gets = jnp.logical_not(first_x), jnp.logical_not(last_x)
        if ds > 0:
            sends = jnp.logical_and(sends, jnp.logical_not(last_y))
            gets = jnp.logical_and(gets, jnp.logical_not(first_y))
        elif ds < 0:
            sends = jnp.logical_and(sends, jnp.logical_not(first_y))
            gets = jnp.logical_and(gets, jnp.logical_not(last_y))
        return sends, gets

    started = []

    def send_near(direction, src, dst, place):
        dv, ds = direction
        copy = pltpu.make_async_remote_copy(
            src_ref=src, dst_ref=dst, send_sem=halo_ss.at[place], recv_sem=halo_rs.at[place],
            device_id=(v + dv, s + ds), device_id_type=MESH,
        )
        sends, gets = each_near(direction)
        pl.when(sends)(copy.start)
        started.append((sends, copy))
        return gets, copy

    def land(gets, copy, put, zero):
        @pl.when(gets)
        def _():
            copy.wait_recv()
            put()

        pl.when(jnp.logical_not(gets))(zero)

    def land_into(pair, dst, src):
        def put():
            dst[...] = src[...].astype(dst.dtype)

        def zero():
            dst[...] = jnp.zeros(dst.shape, dst.dtype)

        land(pair[0], pair[1], put, zero)

    def geo_copy(other, owner):
        return pltpu.make_async_remote_copy(
            src_ref=geo_ref, dst_ref=ge_recv.at[owner], send_sem=ge_ss.at[other],
            recv_sem=ge_rs.at[owner], device_id=device(other), device_id_type=MESH,
        )

    def trace_copy(it, other, owner):
        tile = pl.multiple_of((other // group) * TILE, TILE)
        return pltpu.make_async_remote_copy(
            src_ref=tr_send.at[it, pl.ds(tile, TILE)], dst_ref=tr_recv.at[it, owner],
            send_sem=tr_ss.at[it, other], recv_sem=tr_rs.at[it, owner],
            device_id=(other, s), device_id_type=MESH,
        )

    def density_copy(it, other, owner):
        return pltpu.make_async_remote_copy(
            src_ref=de_send.at[it], dst_ref=de_recv.at[it, owner], send_sem=de_ss.at[it, other],
            recv_sem=de_rs.at[it, owner], device_id=device(other), device_id_type=MESH,
        )

    def others(total, own, body):
        def step(index, carry):
            body(lax.rem(own + index, total))
            return carry

        lax.fori_loop(1, total, step, 0)

    def depth_near(block, low_fill, high_fill):
        up = jnp.where(at_high, high_fill, pltpu.roll(block, depth - 1, 1))
        down = jnp.where(at_low, low_fill, pltpu.roll(block, 1, 1))
        return up, down

    def nu_at(x, y, material):
        center = pe[x + 2, y + 2]
        up, down = depth_near(center, 0.0, 0.0)
        along_x = 0.5 * (pe[x + 3, y + 2] - pe[x + 1, y + 2])
        along_y = 0.5 * (pe[x + 2, y + 3] - pe[x + 2, y + 1])
        along_z = 0.5 * (up - down)
        grad_sq = along_x * along_x + along_y * along_y + along_z * along_z
        base = jnp.zeros(material.shape, jnp.float32)
        slope = jnp.zeros(material.shape, jnp.float32)
        for material_id in range(3):
            picked = material == material_id
            base = jnp.where(picked, NU_BASE[material_id], base)
            slope = jnp.where(picked, NU_SATURATION[material_id], slope)
        return base + slope * grad_sq / (1.0 + grad_sq)

    def all_nu():
        def one_y(y, carry):
            own = []
            for x in range(width_x):
                value = nu_at(x, y, mat_ref[x, pl.ds(y, 1), :])
                nu[x + 1, y + 1] = value
                own.append(value)
            low = nu_at(-1, y, mat_near[0, width_x - 1, pl.ds(y, 1), :])
            high = nu_at(width_x, y, mat_near[1, 0, pl.ds(y, 1), :])
            nu[0, y + 1] = jnp.where(first_x, own[0], low)
            nu[width_x + 1, y + 1] = jnp.where(last_x, own[-1], high)
            return carry

        lax.fori_loop(0, width_y, one_y, 0)
        for x in range(width_x):
            low = nu_at(x, -1, mat_near[2, x, width_y - 1 : width_y, :])
            high = nu_at(x, width_y, mat_near[3, x, 0:1, :])
            nu[x + 1, 0] = jnp.where(first_y, nu[x + 1, 1], low)
            nu[x + 1, width_y + 1] = jnp.where(last_y, nu[x + 1, width_y], high)

    def relaxed(read, x, y):
        own = nu[x + 1, y + 1]
        nu_up, nu_down = depth_near(own, own, own)
        center = read(x, y)
        up, down = depth_near(center, 0.0, 0.0)
        pairs = (
            (nu[x + 2, y + 1], read(x + 1, y)),
            (nu[x, y + 1], read(x - 1, y)),
            (nu[x + 1, y + 2], read(x, y + 1)),
            (nu[x + 1, y], read(x, y - 1)),
            (nu_up, up),
            (nu_down, down),
        )
        diagonal, pulled = None, None
        for near_nu, near in pairs:
            weight = 0.5 * (own + near_nu)
            diagonal = weight if diagonal is None else diagonal + weight
            pulled = weight * near if pulled is None else pulled + weight * near
        applied = diagonal * center - pulled
        return center + RELAXATION * (forcing[x, y] - applied) / diagonal

    def sweep(read, write):
        def one_y(y, carry):
            for x in range(width_x):
                write(x, y, relaxed(read, x, y))
            return carry

        lax.fori_loop(0, width_y, one_y, 0)

    def keep_start(y, carry):
        for x in range(width_x):
            value = start_ref[x, y]
            pe[x + 2, y + 2] = value
            a_send[0, x, y] = value.astype(jnp.bfloat16)
        return carry

    lax.fori_loop(0, width_y, keep_start, 0)
    ge_recv[me] = geo_ref[...]
    pl.semaphore_wait(barrier, count - 1)
    others(count, me, lambda other: geo_copy(other, me).start())

    last_layer = pl.ds(width_x - 1, 1)
    per_iter = 12
    for it in range(ITERS):
        base_sem = it * per_iter
        tr_send[it] = traces_of(
            lambda x, y0: pe[x + 2, 2 + y0 : 2 + y0 + chunk]
        )
        tile = pl.multiple_of((v // group) * TILE, TILE)
        tr_recv[it, v] = tr_send[it, pl.ds(tile, TILE), :]
        others(vol_count, v, lambda other: trace_copy(it, other, v).start())
        if it == 0:
            near_mat = [
                send_near(direction, mat_ref, mat_near.at[k], ITERS * per_iter + k)
                for k, direction in enumerate(((1, 0), (-1, 0), (0, 1), (0, -1)))
            ]
        block = a_send.at[it]
        got_x = [
            send_near((1, 0), block.at[pl.ds(width_x - 2, 2)], ax.at[it, 0], base_sem),
            send_near((-1, 0), block.at[pl.ds(0, 2)], ax.at[it, 1], base_sem + 1),
        ]
        got_y = [
            send_near((0, 1), block.at[:, pl.ds(width_y - 2, 2)], ay.at[it, 0], base_sem + 2),
            send_near((0, -1), block.at[:, pl.ds(0, 2)], ay.at[it, 1], base_sem + 3),
        ]
        got_c = []
        for k, (dv, ds) in enumerate(((1, 1), (1, -1), (-1, 1), (-1, -1))):
            x = width_x - 1 if dv > 0 else 0
            y = width_y - 1 if ds > 0 else 0
            got_c.append(
                send_near((dv, ds), block.at[x, y], ac.at[it, k], base_sem + 4 + k)
            )

        others(vol_count, v, lambda other: trace_copy(it, other, other).wait_recv())
        arrived = tr_recv[it].reshape(vol_count * TILE, LANES).T[:exc_count]
        density = split_dot(arrived, merge_ref[...], NN).astype(jnp.bfloat16)
        de_send[it] = density
        de_recv[it, me] = density
        others(count, me, lambda other: density_copy(it, other, me).start())

        if it == 0:
            others(count, me, lambda other: geo_copy(other, other).wait_recv())
            lanes = lax.broadcasted_iota(jnp.int32, (TILE, LANES), 1)
            mine = jnp.zeros((TILE, LANES), jnp.float32)
            for w in range(vol_count):
                piece = ge_recv[w * src_count]
                for k in range(1, src_count):
                    piece = piece + ge_recv[w * src_count + k]
                ge_all[:, w * LANES : (w + 1) * LANES] = piece
                shift = lax.rem(
                    w * capacity + 2 * LANES - s * slot_count - v * capacity, LANES
                )
                turned = pltpu.roll(piece, shift, 1)
                mine = mine + jnp.where(lanes // capacity == w, turned, 0.0)
            columns = jnp.concatenate([mine] * (LANES // TILE), axis=0).T
            columns = [columns[:, 3 + c : 4 + c] for c in range(3)]
            for w in range(vol_count):
                span = slice(w * LANES, (w + 1) * LANES)
                slot_kernel[:, span] = pair_kernel(
                    columns, [ge_all[c : c + 1, span] for c in range(3)]
                )

        others(count, me, lambda other: density_copy(it, other, other).wait_recv())
        for w in range(vol_count):
            piece = de_recv[it, w * src_count].astype(jnp.float32)
            for k in range(1, src_count):
                piece = piece + de_recv[it, w * src_count + k].astype(jnp.float32)
            dens_all[:, w * LANES : (w + 1) * LANES] = piece.astype(jnp.bfloat16)
        slot_flux = lax.dot_general(
            dens_all[...], slot_kernel[...], NT, preferred_element_type=jnp.float32
        )
        back = slot_flux * flux_scale * slot_scale
        for x in range(width_x):
            for y0 in range(0, width_y, chunk):
                spread = jnp.concatenate(
                    [
                        jnp.where(cell_row == x * width_y + y0 + k, back, 0.0)
                        for k in range(chunk)
                    ],
                    axis=0,
                )
                surface = split_dot(spread, pick_depth, NT)
                for k in range(chunk):
                    forcing[x, y0 + k] = (
                        exc_ref[x, y0 + k] + surface[k * exc_count : (k + 1) * exc_count]
                    )

        if it == 0:
            for k, pair in enumerate(near_mat):
                def zero(k=k):
                    mat_near[k] = jnp.zeros(mat_ref.shape, jnp.int32)

                land(pair[0], pair[1], lambda: None, zero)
        rows, cols = pl.ds(2, width_x), pl.ds(2, width_y)
        land_into(got_y[0], pe.at[rows, pl.ds(0, 2)], ay.at[it, 0])
        land_into(got_y[1], pe.at[rows, pl.ds(width_y + 2, 2)], ay.at[it, 1])
        for k, (dv, ds) in enumerate(((1, 1), (1, -1), (-1, 1), (-1, -1))):
            x = 1 if dv > 0 else width_x + 2
            y = 1 if ds > 0 else width_y + 2
            land_into(got_c[k], pe.at[x, y], ac.at[it, k])
        land_into(got_x[0], pe.at[pl.ds(0, 2), cols], ax.at[it, 0])
        land_into(got_x[1], pe.at[pl.ds(width_x + 2, 2), cols], ax.at[it, 1])
        all_nu()

        def write_first(x, y, value):
            pf[x + 1, y + 1] = value
            b_send[it, x, y] = value.astype(jnp.bfloat16)

        sweep(lambda x, y: pe[x + 2, y + 2], write_first)
        block = b_send.at[it]
        got_x = [
            send_near((1, 0), block.at[last_layer], bx.at[it, 0], base_sem + 8),
            send_near((-1, 0), block.at[pl.ds(0, 1)], bx.at[it, 1], base_sem + 9),
        ]
        got_y = [
            send_near((0, 1), block.at[:, pl.ds(width_y - 1, 1)], by.at[it, 0], base_sem + 10),
            send_near((0, -1), block.at[:, pl.ds(0, 1)], by.at[it, 1], base_sem + 11),
        ]
        if it == ITERS - 1:
            target_block = 256

            def one_block(index, carry):
                span = pl.ds(pl.multiple_of(index * target_block, target_block), target_block)
                points = target_ref[span, :]
                columns = [points[:, c : c + 1] for c in range(3)]
                total = jnp.zeros((target_block, exc_count), jnp.float32)
                for k in range(0, vol_count * LANES, 2 * LANES):
                    part = slice(k, k + 2 * LANES)
                    tile = pair_kernel(columns, [ge_all[c : c + 1, part] for c in range(3)])
                    total = total + lax.dot_general(
                        tile, dens_all[:, part], NT, preferred_element_type=jnp.float32
                    )
                flux_ref[span, :] = total * flux_scale
                return carry

            lax.fori_loop(0, target_ref.shape[0] // target_block, one_block, 0)
        rows, cols = pl.ds(1, width_x), pl.ds(1, width_y)
        land_into(got_y[0], pf.at[rows, pl.ds(0, 1)], by.at[it, 0])
        land_into(got_y[1], pf.at[rows, pl.ds(width_y + 1, 1)], by.at[it, 1])
        land_into(got_x[0], pf.at[pl.ds(0, 1), cols], bx.at[it, 0])
        land_into(got_x[1], pf.at[pl.ds(width_x + 1, 1), cols], bx.at[it, 1])

        def write_second(x, y, value):
            if it == ITERS - 1:
                out_ref[x, y] = value
            else:
                pe[x + 2, y + 2] = value
                a_send[it + 1, x, y] = value.astype(jnp.bfloat16)

        sweep(lambda x, y: pf[x + 1, y + 1], write_second)

    for sends, copy in started:
        pl.when(sends)(copy.wait_send)
    others(count, me, lambda other: geo_copy(other, me).wait_send())
    for it in range(ITERS):
        others(vol_count, v, lambda other: trace_copy(it, other, v).wait_send())
        others(count, me, lambda other: density_copy(it, other, me).wait_send())


def fused(
    excitation, start, material, slot_cells, slot_scale, panels, target_points, source_points,
):
    vol_count, src_count = lax.axis_size("vol"), lax.axis_size("src")
    v, s = lax.axis_index("vol"), lax.axis_index("src")
    exc_count, width_x, width_y, depth = excitation.shape
    slot_count = slot_cells.shape[0]
    capacity = slot_count // vol_count
    piece_len = source_points.shape[1] // vol_count
    group = TILE // capacity
    count = vol_count * src_count

    def lane_rows(rows, fill):
        rows = jnp.stack(rows)
        return jnp.pad(
            rows,
            ((0, TILE - rows.shape[0]), (0, LANES - slot_count)),
            constant_values=fill,
        )

    cells = lane_rows([slot_cells // depth, slot_cells % depth], -1)
    scales = lane_rows([slot_scale], 0.0)
    own_sources = lax.dynamic_slice_in_dim(source_points, v * piece_len, piece_len, 1)
    own_targets = lax.dynamic_slice_in_dim(target_points, s * piece_len, piece_len, 1)
    points = jnp.take(jnp.concatenate([own_sources, own_targets]), panels, axis=1)
    points = jnp.pad(points, ((0, TILE - points.shape[0]), (0, 0)))
    lane_live = jnp.arange(LANES) // slot_count == s
    geometry = jnp.where(lane_live[None, :], jnp.tile(points, (1, src_count)), 0.0)
    order = jnp.arange(slot_count)
    earlier = (panels[:, None] == panels[None, :]) & (order[None, :] < order[:, None])
    lane_panel = jnp.where(jnp.any(earlier, axis=1), -2, panels)
    lane_panel = jnp.where(lane_live, jnp.tile(lane_panel, src_count), -2)
    row_live = (jnp.arange(group) == v % group)[None, :, None]
    row_panel = jnp.where(row_live, panels.reshape(vol_count, 1, capacity), -1).reshape(-1)
    merge = (row_panel[:, None] == lane_panel[None, :]).astype(jnp.bfloat16)

    vmem = pl.BlockSpec(memory_space=pltpu.VMEM)
    field = (width_x, width_y, exc_count, depth)
    plane = (exc_count, depth)
    f32, bf16 = jnp.float32, jnp.bfloat16
    halo_sems = ITERS * 12 + 4
    sources = vol_count * LANES
    dma = pltpu.SemaphoreType.DMA
    potential, flux = pl.pallas_call(
        functools.partial(
            fused_kernel, vol_count, src_count, capacity, float(P_SIZE) ** (-0.5)
        ),
        out_shape=(
            jax.ShapeDtypeStruct(field, f32),
            jax.ShapeDtypeStruct((piece_len, exc_count), f32),
        ),
        in_specs=[vmem] * 8,
        out_specs=(vmem, vmem),
        scratch_shapes=[
            pltpu.VMEM((width_x + 4, width_y + 4) + plane, f32),
            pltpu.VMEM((width_x + 2, width_y + 2) + plane, f32),
            pltpu.VMEM((width_x + 2, width_y + 2) + plane, f32),
            pltpu.VMEM(field, f32),
            pltpu.VMEM((ITERS,) + field, bf16),
            pltpu.VMEM((ITERS, 2, 2, width_y) + plane, bf16),
            pltpu.VMEM((ITERS, 2, width_x, 2) + plane, bf16),
            pltpu.VMEM((ITERS, 4) + plane, bf16),
            pltpu.VMEM((ITERS,) + field, bf16),
            pltpu.VMEM((ITERS, 2, 1, width_y) + plane, bf16),
            pltpu.VMEM((ITERS, 2, width_x, 1) + plane, bf16),
            pltpu.VMEM((4, width_x, width_y, depth), jnp.int32),
            pltpu.VMEM((ITERS, LANES, LANES), f32),
            pltpu.VMEM((ITERS, vol_count, TILE, LANES), f32),
            pltpu.VMEM((ITERS, exc_count, LANES), bf16),
            pltpu.VMEM((ITERS, count, exc_count, LANES), bf16),
            pltpu.VMEM((count, TILE, LANES), f32),
            pltpu.VMEM((TILE, sources), f32),
            pltpu.VMEM((LANES, sources), bf16),
            pltpu.VMEM((exc_count, sources), bf16),
            dma((halo_sems,)),
            dma((halo_sems,)),
            dma((ITERS, vol_count)),
            dma((ITERS, vol_count)),
            dma((ITERS, count)),
            dma((ITERS, count)),
            dma((count,)),
            dma((count,)),
        ],
        compiler_params=pltpu.CompilerParams(
            collective_id=0, has_side_effects=True, vmem_limit_bytes=40 * 1024 * 1024
        ),
    )(
        start.transpose(1, 2, 0, 3),
        excitation.transpose(1, 2, 0, 3),
        material,
        cells,
        scales,
        geometry,
        merge,
        own_targets.T,
    )
    return potential.transpose(2, 0, 1, 3), flux.T


def per_device(
    excitation,
    start,
    material,
    face_cell,
    face_count,
    face_weight,
    slot_panel,
    target_points,
    source_points,
):
    vol_count = lax.axis_size("vol")
    first_x = lax.axis_index("vol") == 0
    last_x = lax.axis_index("vol") == vol_count - 1
    first_y = lax.axis_index("src") == 0
    last_y = lax.axis_index("src") == lax.axis_size("src") - 1
    domain_edges = (first_x, last_x, first_y, last_y)
    exc_count, width_x, width_y, depth_len = excitation.shape
    cell_count = width_x * width_y * depth_len
    slot_cells = face_cell.reshape(-1)
    slot_count = slot_cells.shape[0]
    capacity = slot_count // vol_count
    piece_len = source_points.shape[1] // vol_count
    target_len = target_points.shape[1]
    slot_rank = jnp.arange(slot_count, dtype=jnp.int32) % capacity
    live_count = jnp.repeat(face_count.reshape(-1), capacity, total_repeat_length=slot_count)
    slot_scale = jnp.where(slot_rank < live_count, face_weight.reshape(-1), 0.0)
    lane_tile = LANES == depth_len == slot_count * lax.axis_size("src")
    if (
        lane_tile
        and vol_count * TILE == LANES
        and TILE % capacity == 0
        and LANES % exc_count == 0
        and exc_count % 16 == 0
        and width_x >= 2
        and width_y % 8 == 0
        and piece_len % 256 == 0
        and piece_len * lax.axis_size("src") == target_len
    ):
        return fused(
            excitation, start, material, slot_cells, slot_scale, slot_panel.reshape(-1),
            target_points, source_points,
        )
    compact = slot_count < piece_len
    vol_index = lax.axis_index("vol")
    src_index = lax.axis_index("src")
    src_count = lax.axis_size("src")
    panels = slot_panel.reshape(-1)
    if compact:
        own_points = jnp.concatenate(
            [
                jnp.take(lax.dynamic_slice_in_dim(source_points, vol_index * piece_len, piece_len, 1), panels, axis=1),
                jnp.take(lax.dynamic_slice_in_dim(target_points, src_index * piece_len, piece_len, 1), panels, axis=1),
                panels.astype(jnp.float32)[None],
            ]
        )
        own_targets = lax.dynamic_slice_in_dim(target_points, src_index * piece_len, piece_len, 1)
    else:
        owner_table = (
            panels[:, None] == jnp.arange(piece_len, dtype=jnp.int32)[None, :]
        ).astype(jnp.float32)
    flux_scale = float(P_SIZE) ** (-0.5)
    potential = start
    flux_own = jnp.zeros((exc_count, piece_len), jnp.float32)
    for outer_index in range(ITERS):
        current = with_rim(potential)
        nu_own = reluctivity(gradient_sq(pad_depth(current)), material)
        nu_ext = extended(nu_own, (("vol", 1), ("src", 2)), 1)
        weights = face_weights(nu_ext, domain_edges)
        diagonal = weights[0] + weights[1] + weights[2] + weights[3] + weights[4] + weights[5]
        cell_values = jnp.take(potential.reshape(exc_count, cell_count), slot_cells, axis=1)
        if compact:
            traces = (cell_values * slot_scale[None, :]).T
            message = traces if outer_index else jnp.concatenate([traces, own_points.T], axis=1)
            gathered = lax.all_gather(message, ("vol", "src"), axis=0, tiled=False)
            gathered = gathered.reshape(vol_count, src_count, slot_count, -1)
            if outer_index == 0:
                points = gathered[..., exc_count:]
                places = points[..., :3].reshape(-1, 3).T
                ids = points[..., 6]
                same = ids[..., :, None] == ids[..., None, :]
                rank = jnp.arange(slot_count)
                earlier = same & (rank[None, :] < rank[:, None])
                merge = (same & ~jnp.any(earlier, axis=-1)[..., None]).astype(jnp.float32)
                mine = lax.dynamic_index_in_dim(points, src_index, 1, keepdims=False)
                mine = mine.reshape(vol_count, vol_count, capacity, -1)
                mine = lax.dynamic_index_in_dim(mine, vol_index, 1, keepdims=False)
                slot_targets = mine[..., 3:6].reshape(-1, 3).T
                slot_kernel = kernel_block(slot_targets, places)
            arrived = gathered[..., :exc_count].reshape(
                vol_count, src_count, vol_count, capacity, exc_count
            )
            arrived = arrived.transpose(2, 1, 0, 3, 4).reshape(
                vol_count, src_count, slot_count, exc_count
            )
            density = jnp.einsum(
                "wsij,wsje->wsie", merge, arrived, precision=lax.Precision.HIGHEST
            )
            density = density.reshape(-1, exc_count).astype(jnp.bfloat16)
            returned = flux_scale * jnp.einsum(
                "tn,ne->te", slot_kernel, density, preferred_element_type=jnp.float32
            )
            if outer_index == ITERS - 1:
                flux_own = flux_scale * jnp.einsum(
                    "ne,tn->et",
                    density,
                    kernel_block(own_targets, places),
                    preferred_element_type=jnp.float32,
                )
        else:
            outgoing = (cell_values * slot_scale[None, :]).T.reshape(vol_count, capacity * exc_count)
            arrived = lax.all_to_all(outgoing, "vol", split_axis=0, concat_axis=0, tiled=True).reshape(
                slot_count, exc_count
            )
            density = jnp.dot(
                arrived.T,
                owner_table,
                precision=lax.Precision.HIGHEST,
                preferred_element_type=jnp.float32,
            ).astype(jnp.bfloat16)
            block_piece = lax.all_gather(density, "vol", axis=1, tiled=True)
            piece_count = block_piece.shape[1]
            step_len = 1024

            def one_step(step_index, partial_value):
                offset_index = step_index * step_len
                segment = lax.dynamic_slice_in_dim(block_piece, offset_index, step_len, 1)
                places = lax.dynamic_slice_in_dim(source_points, offset_index, step_len, 1)
                dist_sq = jnp.zeros((target_len, step_len), jnp.float32)
                for component in range(3):
                    offset = target_points[component][:, None] - places[component][None, :]
                    dist_sq = dist_sq + offset * offset
                kernel = lax.rsqrt(dist_sq + SOFTENING * SOFTENING).astype(jnp.bfloat16)
                return partial_value + jnp.einsum(
                    "en,tn->et", segment, kernel, preferred_element_type=jnp.float32
                )

            partial_flux = lax.fori_loop(
                0, piece_count // step_len, one_step, jnp.zeros((exc_count, target_len), jnp.float32)
            )
            flux_sum = lax.psum_scatter(partial_flux, "src", scatter_dimension=1, tiled=True)
            flux_own = flux_sum * flux_scale
            per_slot = jnp.dot(
                flux_own,
                owner_table.T,
                precision=lax.Precision.HIGHEST,
                preferred_element_type=jnp.float32,
            )
            returned = lax.all_to_all(
                per_slot.T.reshape(vol_count, capacity * exc_count),
                "vol",
                split_axis=0,
                concat_axis=0,
                tiled=True,
            ).reshape(slot_count, exc_count)
        contribution = returned.T * slot_scale[None, :]
        surface = (
            jnp.zeros((exc_count, cell_count), jnp.float32).at[:, slot_cells].add(contribution)
        )
        forcing = excitation + surface.reshape(excitation.shape)
        for sweep_index in range(SWEEPS):
            if sweep_index > 0:
                current = with_rim(potential)
            potential = relax(pad_depth(current), weights, diagonal, forcing)
    return (potential, flux_own)


def solution(mesh):
    return jax.shard_map(
        per_device,
        mesh=mesh,
        in_specs=(
            P(None, "vol", "src", None),
            P(None, "vol", "src", None),
            P("vol", "src", None),
            P("vol", "src", None),
            P("vol", "src", None),
            P("vol", "src", None),
            P("vol", "src", None),
            P(None, "vol"),
            P(None, "src"),
        ),
        out_specs=(P(None, "vol", "src", None), P(None, ("vol", "src"))),
        check_vma=False,
    )
```

```python
import functools

import jax
import jax.numpy as jnp
from jax import lax
from jax.experimental import pallas as pl
from jax.experimental.pallas import tpu as pltpu
from jax.sharding import PartitionSpec as P

P_SIZE = 65536
ITERS = 2
SWEEPS = 2


NU_BASE = (1.0, 0.05, 0.4)
NU_SATURATION = (0.0, 0.9, 0.3)
RELAXATION = 0.8
SOFTENING = 0.05


def extended(block, sides, width):
    for axis, dim in sides:
        count = lax.axis_size(axis)
        forward = [(i, i + 1) for i in range(count - 1)]
        backward = [(target, source) for source, target in forward]
        low = lax.ppermute(
            lax.slice_in_dim(block, block.shape[dim] - width, None, axis=dim), axis, forward
        )
        high = lax.ppermute(lax.slice_in_dim(block, 0, width, axis=dim), axis, backward)
        block = jnp.concatenate([low, block, high], axis=dim)
    return block


def reluctivity(grad_sq, material):
    base_value = jnp.zeros(material.shape, jnp.float32)
    slope_value = jnp.zeros(material.shape, jnp.float32)
    for material_id in range(3):
        picked = material == material_id
        base_value = jnp.where(picked, NU_BASE[material_id], base_value)
        slope_value = jnp.where(picked, NU_SATURATION[material_id], slope_value)
    return base_value[None] + slope_value[None] * grad_sq / (1.0 + grad_sq)


def gradient_sq(padded):
    along_x = 0.5 * (padded[:, 2:, 1:-1, 1:-1] - padded[:, :-2, 1:-1, 1:-1])
    along_y = 0.5 * (padded[:, 1:-1, 2:, 1:-1] - padded[:, 1:-1, :-2, 1:-1])
    along_z = 0.5 * (padded[:, 1:-1, 1:-1, 2:] - padded[:, 1:-1, 1:-1, :-2])
    return along_x * along_x + along_y * along_y + along_z * along_z


def pad_depth(values):
    return jnp.pad(values, ((0, 0), (0, 0), (0, 0), (1, 1)))


def face_weights(nu_ext, domain_edges):
    first_x, last_x, first_y, last_y = domain_edges
    interior = nu_ext[:, 1:-1, 1:-1]
    low_x = jnp.where(first_x, interior[:, :1], nu_ext[:, :1, 1:-1])
    high_x = jnp.where(last_x, interior[:, -1:], nu_ext[:, -1:, 1:-1])
    column = jnp.concatenate([low_x, interior, high_x], axis=1)
    low_y = jnp.where(first_y, interior[:, :, :1], nu_ext[:, 1:-1, :1])
    high_y = jnp.where(last_y, interior[:, :, -1:], nu_ext[:, 1:-1, -1:])
    row_ext = jnp.concatenate([low_y, interior, high_y], axis=2)
    depth_ext = jnp.pad(interior, ((0, 0), (0, 0), (0, 0), (1, 1)), mode="edge")
    return (
        0.5 * (interior + column[:, 2:]),
        0.5 * (interior + column[:, :-2]),
        0.5 * (interior + row_ext[:, :, 2:]),
        0.5 * (interior + row_ext[:, :, :-2]),
        0.5 * (interior + depth_ext[:, :, :, 2:]),
        0.5 * (interior + depth_ext[:, :, :, :-2]),
    )


def relax(padded, weights, diagonal, forcing):
    center = padded[:, 1:-1, 1:-1, 1:-1]
    neighbours = (
        padded[:, 2:, 1:-1, 1:-1],
        padded[:, :-2, 1:-1, 1:-1],
        padded[:, 1:-1, 2:, 1:-1],
        padded[:, 1:-1, :-2, 1:-1],
        padded[:, 1:-1, 1:-1, 2:],
        padded[:, 1:-1, 1:-1, :-2],
    )
    applied = diagonal * center
    for weight, neighbour in zip(weights, neighbours):
        applied = applied - weight * neighbour
    return center + RELAXATION * (forcing - applied) / diagonal


def kernel_block(targets, places):
    dist_sq = jnp.zeros((targets.shape[1], places.shape[1]), jnp.float32)
    for component in range(3):
        offset = targets[component][:, None] - places[component][None, :]
        dist_sq = dist_sq + offset * offset
    return lax.rsqrt(dist_sq + SOFTENING * SOFTENING).astype(jnp.bfloat16)


def with_rim(potential):
    return extended(potential, (("vol", 1), ("src", 2)), 1)


MESH = pl.DeviceIdType.MESH
LANES = 128
TILE = 8
NT = (((1,), (1,)), ((), ()))
NN = (((1,), (0,)), ((), ()))


def split_dot(values, selector, dims):
    total = None
    for _ in range(3):
        part = values.astype(jnp.bfloat16)
        term = lax.dot_general(part, selector, dims, preferred_element_type=jnp.float32)
        total = term if total is None else total + term
        values = values - part.astype(jnp.float32)
    return total


def one_hot(mask):
    return jnp.where(mask, 1.0, 0.0).astype(jnp.bfloat16)


def as_columns(rows):
    return jnp.concatenate([rows] * (LANES // rows.shape[0]), axis=0).T


def pair_kernel(columns, rows):
    dist_sq = None
    for column, row in zip(columns, rows):
        offset = column - row
        dist_sq = offset * offset if dist_sq is None else dist_sq + offset * offset
    return lax.rsqrt(dist_sq + SOFTENING * SOFTENING).astype(jnp.bfloat16)


def fused_kernel(
    vol_count, src_count, capacity, flux_scale,
    start_ref, exc_ref, mat_ref, cell_ref, live_ref, weight_ref, panel_ref, target_ref, source_ref,
    out_ref, flux_ref,
    pe, pf, nu, forcing, a_send, ax, ay, ac, b_send, bx, by, mat_near,
    tr_send, tr_recv, de_send, de_recv, ge_recv, ge_all, slot_kernel, dens_all,
    points_ref, geo_ref, halo_ss, halo_rs, tr_ss, tr_rs, de_ss, de_rs, ge_ss, ge_rs,
):
    width_x, width_y, exc_count, depth = start_ref.shape
    count = vol_count * src_count
    v, s = lax.axis_index("vol"), lax.axis_index("src")
    me = v * src_count + s
    group = TILE // capacity
    slot_count = vol_count * capacity
    first_x, last_x = v == 0, v == vol_count - 1
    first_y, last_y = s == 0, s == src_count - 1

    def device(index):
        return (index // src_count, lax.rem(index, src_count))

    barrier = pltpu.get_barrier_semaphore()

    def greet(step, carry):
        other = lax.rem(me + step, count)
        pl.semaphore_signal(barrier, inc=1, device_id=device(other), device_id_type=MESH)
        return carry

    lax.fori_loop(1, count, greet, 0)

    lane = lax.broadcasted_iota(jnp.int32, (exc_count, depth), 1)
    at_low, at_high = lane == 0, lane == depth - 1
    row64 = lax.broadcasted_iota(jnp.int32, (slot_count, LANES), 0)
    lane64 = lax.broadcasted_iota(jnp.int32, (slot_count, LANES), 1)
    repeat_slots = one_hot(lane64 % slot_count == row64)

    def spread_rows(ref, selector):
        values = jnp.broadcast_to(ref[...].astype(jnp.float32), (TILE, ref.shape[1]))
        return split_dot(values, selector, NN)

    lane_row = lax.broadcasted_iota(jnp.int32, (1, LANES), 1)
    lane_owner = lax.broadcasted_iota(jnp.int32, (vol_count, LANES), 1) % slot_count // capacity
    pick_owner = one_hot(
        lane_owner == lax.broadcasted_iota(jnp.int32, (vol_count, LANES), 0)
    )
    slot_cell = spread_rows(cell_ref, repeat_slots)[0:1].astype(jnp.int32)
    slot_cell = jnp.where(lane_row < slot_count, slot_cell, -1)
    cell_row = slot_cell >> (depth.bit_length() - 1)
    cell_depth = jnp.where(slot_cell < 0, -1, slot_cell & (depth - 1))
    live = (lane_row % capacity).astype(jnp.float32) < spread_rows(live_ref, pick_owner)[0:1]
    slot_scale = jnp.where(
        live & (lane_row < slot_count), spread_rows(weight_ref, repeat_slots)[0:1], 0.0
    )
    pick_depth = one_hot(lax.broadcasted_iota(jnp.int32, (depth, LANES), 0) == cell_depth)
    chunk = 8

    def traces_of(read):
        total = jnp.zeros((exc_count, LANES), jnp.float32)
        for x in range(width_x):
            for y0 in range(0, width_y, chunk):
                block = read(x, y0).reshape(chunk * exc_count, depth)
                taken = split_dot(block, pick_depth, NN)
                for k in range(chunk):
                    row = x * width_y + y0 + k
                    total = total + jnp.where(
                        cell_row == row, taken[k * exc_count : (k + 1) * exc_count], 0.0
                    )
        total = total * slot_scale
        return as_columns(total)

    def each_near(direction):
        dv, ds = direction
        sends, gets = True, True
        if dv > 0:
            sends, gets = jnp.logical_not(last_x), jnp.logical_not(first_x)
        elif dv < 0:
            sends, gets = jnp.logical_not(first_x), jnp.logical_not(last_x)
        if ds > 0:
            sends = jnp.logical_and(sends, jnp.logical_not(last_y))
            gets = jnp.logical_and(gets, jnp.logical_not(first_y))
        elif ds < 0:
            sends = jnp.logical_and(sends, jnp.logical_not(first_y))
            gets = jnp.logical_and(gets, jnp.logical_not(last_y))
        return sends, gets

    started = []

    def send_near(direction, src, dst, place):
        dv, ds = direction
        copy = pltpu.make_async_remote_copy(
            src_ref=src, dst_ref=dst, send_sem=halo_ss.at[place], recv_sem=halo_rs.at[place],
            device_id=(v + dv, s + ds), device_id_type=MESH,
        )
        sends, gets = each_near(direction)
        pl.when(sends)(copy.start)
        started.append((sends, copy))
        return gets, copy

    def land(gets, copy, put, zero):
        @pl.when(gets)
        def _():
            copy.wait_recv()
            put()

        pl.when(jnp.logical_not(gets))(zero)

    def land_into(pair, dst, src):
        def put():
            dst[...] = src[...].astype(dst.dtype)

        def zero():
            dst[...] = jnp.zeros(dst.shape, dst.dtype)

        land(pair[0], pair[1], put, zero)

    def geo_copy(other, owner):
        return pltpu.make_async_remote_copy(
            src_ref=geo_ref, dst_ref=ge_recv.at[owner], send_sem=ge_ss.at[other],
            recv_sem=ge_rs.at[owner], device_id=device(other), device_id_type=MESH,
        )

    def trace_copy(it, other, owner):
        tile = pl.multiple_of((other // group) * TILE, TILE)
        return pltpu.make_async_remote_copy(
            src_ref=tr_send.at[it, pl.ds(tile, TILE)], dst_ref=tr_recv.at[it, owner],
            send_sem=tr_ss.at[it, other], recv_sem=tr_rs.at[it, owner],
            device_id=(other, s), device_id_type=MESH,
        )

    def density_copy(it, other, owner):
        return pltpu.make_async_remote_copy(
            src_ref=de_send.at[it], dst_ref=de_recv.at[it, owner], send_sem=de_ss.at[it, other],
            recv_sem=de_rs.at[it, owner], device_id=device(other), device_id_type=MESH,
        )

    def others(total, own, body):
        def step(index, carry):
            body(lax.rem(own + index, total))
            return carry

        lax.fori_loop(1, total, step, 0)

    def each_y(body):
        def some(index, carry):
            for k in range(4):
                body(index * 4 + k)
            return carry

        lax.fori_loop(0, width_y // 4, some, 0)

    def depth_near(block, low_fill, high_fill):
        up = jnp.where(at_high, high_fill, pltpu.roll(block, depth - 1, 1))
        down = jnp.where(at_low, low_fill, pltpu.roll(block, 1, 1))
        return up, down

    def nu_at(x, y, material):
        center = pe[x + 2, y + 2]
        up, down = depth_near(center, 0.0, 0.0)
        along_x = 0.5 * (pe[x + 3, y + 2] - pe[x + 1, y + 2])
        along_y = 0.5 * (pe[x + 2, y + 3] - pe[x + 2, y + 1])
        along_z = 0.5 * (up - down)
        grad_sq = along_x * along_x + along_y * along_y + along_z * along_z
        base = jnp.zeros(material.shape, jnp.float32)
        slope = jnp.zeros(material.shape, jnp.float32)
        for material_id in range(3):
            picked = material == material_id
            base = jnp.where(picked, NU_BASE[material_id], base)
            slope = jnp.where(picked, NU_SATURATION[material_id], slope)
        return base + slope * grad_sq / (1.0 + grad_sq)

    def all_nu():
        def one_y(y):
            own = []
            for x in range(width_x):
                value = nu_at(x, y, mat_ref[x, pl.ds(y, 1), :])
                nu[x + 1, y + 1] = value
                own.append(value)
            low = nu_at(-1, y, mat_near[0, width_x - 1, pl.ds(y, 1), :])
            high = nu_at(width_x, y, mat_near[1, 0, pl.ds(y, 1), :])
            nu[0, y + 1] = jnp.where(first_x, own[0], low)
            nu[width_x + 1, y + 1] = jnp.where(last_x, own[-1], high)

        each_y(one_y)
        for x in range(width_x):
            low = nu_at(x, -1, mat_near[2, x, width_y - 1 : width_y, :])
            high = nu_at(x, width_y, mat_near[3, x, 0:1, :])
            nu[x + 1, 0] = jnp.where(first_y, nu[x + 1, 1], low)
            nu[x + 1, width_y + 1] = jnp.where(last_y, nu[x + 1, width_y], high)

    def relaxed(read, x, y):
        own = nu[x + 1, y + 1]
        nu_up, nu_down = depth_near(own, own, own)
        center = read(x, y)
        up, down = depth_near(center, 0.0, 0.0)
        pairs = (
            (nu[x + 2, y + 1], read(x + 1, y)),
            (nu[x, y + 1], read(x - 1, y)),
            (nu[x + 1, y + 2], read(x, y + 1)),
            (nu[x + 1, y], read(x, y - 1)),
            (nu_up, up),
            (nu_down, down),
        )
        diagonal, pulled = None, None
        for near_nu, near in pairs:
            weight = 0.5 * (own + near_nu)
            diagonal = weight if diagonal is None else diagonal + weight
            pulled = weight * near if pulled is None else pulled + weight * near
        applied = diagonal * center - pulled
        return center + RELAXATION * (forcing[x, y] - applied) / diagonal

    def sweep(read, write):
        def one_y(y):
            for x in range(width_x):
                write(x, y, relaxed(read, x, y))

        each_y(one_y)

    def keep_start(y):
        for x in range(width_x):
            value = start_ref[x, y]
            pe[x + 2, y + 2] = value
            a_send[0, x, y] = value.astype(jnp.bfloat16)

    each_y(keep_start)

    def place_points():
        piece_len = points_ref.shape[1]
        points_ref[0:3, :] = source_ref[
            :, pl.ds(pl.multiple_of(v * piece_len, LANES), piece_len)
        ]
        points_ref[3:6, :] = target_ref[
            :, pl.ds(pl.multiple_of(s * piece_len, LANES), piece_len)
        ]
        points_ref[6:8, :] = jnp.zeros((2, piece_len), jnp.float32)
        lane_panel = spread_rows(panel_ref, repeat_slots)
        lane_index = lane_panel[0:1].astype(jnp.int32)
        total = jnp.zeros((TILE, LANES), jnp.float32)
        step = 256
        for k in range(0, piece_len, step):
            index = lax.broadcasted_iota(jnp.int32, (step, LANES), 0) + k
            total = total + split_dot(
                points_ref[:, k : k + step], one_hot(index == lane_index), NN
            )
        lane_live = lane_row // slot_count == s
        geo_ref[...] = jnp.where(lane_live, total, 0.0)
        row = lax.broadcasted_iota(jnp.int32, (LANES, LANES), 0)
        column = lax.broadcasted_iota(jnp.int32, (LANES, LANES), 1)
        earlier = (as_columns(lane_panel) == lane_panel[0:1]) & (row < column % slot_count)
        repeated = jnp.sum(jnp.where(earlier, 1.0, 0.0), axis=0, keepdims=True)
        arrival_slot = lane64 // TILE * capacity + lane64 % capacity
        row_panel = as_columns(spread_rows(panel_ref, one_hot(arrival_slot == row64)))
        keep = (row_panel == lane_panel[0:1]) & (repeated == 0.0) & lane_live
        return one_hot(keep & (row % TILE // capacity == lax.rem(v, group)))

    last_layer = pl.ds(width_x - 1, 1)
    per_iter = 12
    for it in range(ITERS):
        base_sem = it * per_iter
        tr_send[it] = traces_of(
            lambda x, y0: pe[x + 2, 2 + y0 : 2 + y0 + chunk]
        )
        tile = pl.multiple_of((v // group) * TILE, TILE)
        tr_recv[it, v] = tr_send[it, pl.ds(tile, TILE), :]
        if it == 0:
            pl.semaphore_wait(barrier, count - 1)
        others(vol_count, v, lambda other: trace_copy(it, other, v).start())
        if it == 0:
            near_mat = [
                send_near(direction, mat_ref, mat_near.at[k], ITERS * per_iter + k)
                for k, direction in enumerate(((1, 0), (-1, 0), (0, 1), (0, -1)))
            ]
        block = a_send.at[it]
        got_x = [
            send_near((1, 0), block.at[pl.ds(width_x - 2, 2)], ax.at[it, 0], base_sem),
            send_near((-1, 0), block.at[pl.ds(0, 2)], ax.at[it, 1], base_sem + 1),
        ]
        got_y = [
            send_near((0, 1), block.at[:, pl.ds(width_y - 2, 2)], ay.at[it, 0], base_sem + 2),
            send_near((0, -1), block.at[:, pl.ds(0, 2)], ay.at[it, 1], base_sem + 3),
        ]
        got_c = []
        for k, (dv, ds) in enumerate(((1, 1), (1, -1), (-1, 1), (-1, -1))):
            x = width_x - 1 if dv > 0 else 0
            y = width_y - 1 if ds > 0 else 0
            got_c.append(
                send_near((dv, ds), block.at[x, y], ac.at[it, k], base_sem + 4 + k)
            )

        if it == 0:
            merge = place_points()
            ge_recv[me] = geo_ref[...]
            others(count, me, lambda other: geo_copy(other, me).start())
        others(vol_count, v, lambda other: trace_copy(it, other, other).wait_recv())
        arrived = tr_recv[it].reshape(vol_count * TILE, LANES).T[:exc_count]
        density = split_dot(arrived, merge, NN).astype(jnp.bfloat16)
        de_send[it] = density
        de_recv[it, me] = density
        others(count, me, lambda other: density_copy(it, other, me).start())

        if it == 0:
            others(count, me, lambda other: geo_copy(other, other).wait_recv())
            lanes = lax.broadcasted_iota(jnp.int32, (TILE, LANES), 1)
            mine = jnp.zeros((TILE, LANES), jnp.float32)
            for w in range(vol_count):
                piece = ge_recv[w * src_count]
                for k in range(1, src_count):
                    piece = piece + ge_recv[w * src_count + k]
                ge_all[:, w * LANES : (w + 1) * LANES] = piece
                shift = lax.rem(
                    w * capacity + 2 * LANES - s * slot_count - v * capacity, LANES
                )
                turned = pltpu.roll(piece, shift, 1)
                mine = mine + jnp.where(lanes // capacity == w, turned, 0.0)
            columns = as_columns(mine)
            columns = [columns[:, 3 + c : 4 + c] for c in range(3)]
            for w in range(vol_count):
                span = slice(w * LANES, (w + 1) * LANES)
                slot_kernel[:, span] = pair_kernel(
                    columns, [ge_all[c : c + 1, span] for c in range(3)]
                )

        others(count, me, lambda other: density_copy(it, other, other).wait_recv())
        for w in range(vol_count):
            piece = de_recv[it, w * src_count].astype(jnp.float32)
            for k in range(1, src_count):
                piece = piece + de_recv[it, w * src_count + k].astype(jnp.float32)
            dens_all[:, w * LANES : (w + 1) * LANES] = piece.astype(jnp.bfloat16)
        slot_flux = lax.dot_general(
            dens_all[...], slot_kernel[...], NT, preferred_element_type=jnp.float32
        )
        back = slot_flux * flux_scale * slot_scale
        for x in range(width_x):
            for y0 in range(0, width_y, chunk):
                spread = jnp.concatenate(
                    [
                        jnp.where(cell_row == x * width_y + y0 + k, back, 0.0)
                        for k in range(chunk)
                    ],
                    axis=0,
                )
                surface = split_dot(spread, pick_depth, NT)
                for k in range(chunk):
                    forcing[x, y0 + k] = (
                        exc_ref[x, y0 + k] + surface[k * exc_count : (k + 1) * exc_count]
                    )

        if it == 0:
            for k, pair in enumerate(near_mat):
                def zero(k=k):
                    mat_near[k] = jnp.zeros(mat_ref.shape, jnp.int32)

                land(pair[0], pair[1], lambda: None, zero)
        rows, cols = pl.ds(2, width_x), pl.ds(2, width_y)
        land_into(got_y[0], pe.at[rows, pl.ds(0, 2)], ay.at[it, 0])
        land_into(got_y[1], pe.at[rows, pl.ds(width_y + 2, 2)], ay.at[it, 1])
        for k, (dv, ds) in enumerate(((1, 1), (1, -1), (-1, 1), (-1, -1))):
            x = 1 if dv > 0 else width_x + 2
            y = 1 if ds > 0 else width_y + 2
            land_into(got_c[k], pe.at[x, y], ac.at[it, k])
        land_into(got_x[0], pe.at[pl.ds(0, 2), cols], ax.at[it, 0])
        land_into(got_x[1], pe.at[pl.ds(width_x + 2, 2), cols], ax.at[it, 1])
        all_nu()

        def write_first(x, y, value):
            pf[x + 1, y + 1] = value
            b_send[it, x, y] = value.astype(jnp.bfloat16)

        sweep(lambda x, y: pe[x + 2, y + 2], write_first)
        block = b_send.at[it]
        got_x = [
            send_near((1, 0), block.at[last_layer], bx.at[it, 0], base_sem + 8),
            send_near((-1, 0), block.at[pl.ds(0, 1)], bx.at[it, 1], base_sem + 9),
        ]
        got_y = [
            send_near((0, 1), block.at[:, pl.ds(width_y - 1, 1)], by.at[it, 0], base_sem + 10),
            send_near((0, -1), block.at[:, pl.ds(0, 1)], by.at[it, 1], base_sem + 11),
        ]
        if it == ITERS - 1:
            target_block = 256

            def one_block(index, carry):
                span = pl.ds(pl.multiple_of(index * target_block, target_block), target_block)
                points = jnp.concatenate(
                    [
                        as_columns(
                            points_ref[
                                :,
                                pl.ds(
                                    pl.multiple_of(index * target_block + k, LANES), LANES
                                ),
                            ]
                        )
                        for k in range(0, target_block, LANES)
                    ],
                    axis=0,
                )
                columns = [points[:, 3 + c : 4 + c] for c in range(3)]
                total = jnp.zeros((target_block, exc_count), jnp.float32)
                for k in range(0, vol_count * LANES, 2 * LANES):
                    part = slice(k, k + 2 * LANES)
                    tile = pair_kernel(columns, [ge_all[c : c + 1, part] for c in range(3)])
                    total = total + lax.dot_general(
                        tile, dens_all[:, part], NT, preferred_element_type=jnp.float32
                    )
                flux_ref[span, :] = total * flux_scale
                return carry

            lax.fori_loop(0, points_ref.shape[1] // target_block, one_block, 0)
        rows, cols = pl.ds(1, width_x), pl.ds(1, width_y)
        land_into(got_y[0], pf.at[rows, pl.ds(0, 1)], by.at[it, 0])
        land_into(got_y[1], pf.at[rows, pl.ds(width_y + 1, 1)], by.at[it, 1])
        land_into(got_x[0], pf.at[pl.ds(0, 1), cols], bx.at[it, 0])
        land_into(got_x[1], pf.at[pl.ds(width_x + 1, 1), cols], bx.at[it, 1])

        def write_second(x, y, value):
            if it == ITERS - 1:
                out_ref[x, y] = value
            else:
                pe[x + 2, y + 2] = value
                a_send[it + 1, x, y] = value.astype(jnp.bfloat16)

        sweep(lambda x, y: pf[x + 1, y + 1], write_second)

    for sends, copy in started:
        pl.when(sends)(copy.wait_send)
    others(count, me, lambda other: geo_copy(other, me).wait_send())
    for it in range(ITERS):
        others(vol_count, v, lambda other: trace_copy(it, other, v).wait_send())
        others(count, me, lambda other: density_copy(it, other, me).wait_send())


def fused(
    excitation, start, material, face_cell, face_count, face_weight, slot_panel,
    target_points, source_points,
):
    vol_count, src_count = lax.axis_size("vol"), lax.axis_size("src")
    exc_count, width_x, width_y, depth = excitation.shape
    slot_count = face_cell.size
    capacity = slot_count // vol_count
    piece_len = source_points.shape[1] // vol_count
    count = vol_count * src_count
    vmem = pl.BlockSpec(memory_space=pltpu.VMEM)
    field = (width_x, width_y, exc_count, depth)
    plane = (exc_count, depth)
    f32, bf16 = jnp.float32, jnp.bfloat16
    halo_sems = ITERS * 12 + 4
    sources = vol_count * LANES
    dma = pltpu.SemaphoreType.DMA
    potential, flux = pl.pallas_call(
        functools.partial(
            fused_kernel, vol_count, src_count, capacity, float(P_SIZE) ** (-0.5)
        ),
        out_shape=(
            jax.ShapeDtypeStruct(field, f32),
            jax.ShapeDtypeStruct((piece_len, exc_count), f32),
        ),
        in_specs=[vmem] * 9,
        out_specs=(vmem, vmem),
        scratch_shapes=[
            pltpu.VMEM((width_x + 4, width_y + 4) + plane, f32),
            pltpu.VMEM((width_x + 2, width_y + 2) + plane, f32),
            pltpu.VMEM((width_x + 2, width_y + 2) + plane, f32),
            pltpu.VMEM(field, f32),
            pltpu.VMEM((ITERS,) + field, bf16),
            pltpu.VMEM((ITERS, 2, 2, width_y) + plane, bf16),
            pltpu.VMEM((ITERS, 2, width_x, 2) + plane, bf16),
            pltpu.VMEM((ITERS, 4) + plane, bf16),
            pltpu.VMEM((ITERS,) + field, bf16),
            pltpu.VMEM((ITERS, 2, 1, width_y) + plane, bf16),
            pltpu.VMEM((ITERS, 2, width_x, 1) + plane, bf16),
            pltpu.VMEM((4, width_x, width_y, depth), jnp.int32),
            pltpu.VMEM((ITERS, LANES, LANES), f32),
            pltpu.VMEM((ITERS, vol_count, TILE, LANES), f32),
            pltpu.VMEM((ITERS, exc_count, LANES), bf16),
            pltpu.VMEM((ITERS, count, exc_count, LANES), bf16),
            pltpu.VMEM((count, TILE, LANES), f32),
            pltpu.VMEM((TILE, sources), f32),
            pltpu.VMEM((LANES, sources), bf16),
            pltpu.VMEM((exc_count, sources), bf16),
            pltpu.VMEM((TILE, piece_len), f32),
            pltpu.VMEM((TILE, LANES), f32),
            dma((halo_sems,)),
            dma((halo_sems,)),
            dma((ITERS, vol_count)),
            dma((ITERS, vol_count)),
            dma((ITERS, count)),
            dma((ITERS, count)),
            dma((count,)),
            dma((count,)),
        ],
        compiler_params=pltpu.CompilerParams(
            collective_id=0, has_side_effects=True, vmem_limit_bytes=40 * 1024 * 1024
        ),
    )(
        start.transpose(1, 2, 0, 3),
        excitation.transpose(1, 2, 0, 3),
        material,
        face_cell.reshape(1, -1),
        face_count.reshape(1, -1),
        face_weight.reshape(1, -1),
        slot_panel.reshape(1, -1),
        target_points,
        source_points,
    )
    return potential.transpose(2, 0, 1, 3), flux.T


def per_device(
    excitation,
    start,
    material,
    face_cell,
    face_count,
    face_weight,
    slot_panel,
    target_points,
    source_points,
):
    vol_count = lax.axis_size("vol")
    first_x = lax.axis_index("vol") == 0
    last_x = lax.axis_index("vol") == vol_count - 1
    first_y = lax.axis_index("src") == 0
    last_y = lax.axis_index("src") == lax.axis_size("src") - 1
    domain_edges = (first_x, last_x, first_y, last_y)
    exc_count, width_x, width_y, depth_len = excitation.shape
    cell_count = width_x * width_y * depth_len
    slot_cells = face_cell.reshape(-1)
    slot_count = slot_cells.shape[0]
    capacity = slot_count // vol_count
    piece_len = source_points.shape[1] // vol_count
    target_len = target_points.shape[1]
    lane_tile = LANES == depth_len == slot_count * lax.axis_size("src")
    if (
        lane_tile
        and vol_count * TILE == LANES
        and TILE % capacity == 0
        and LANES % exc_count == 0
        and exc_count % 16 == 0
        and width_x >= 2
        and width_y % 8 == 0
        and piece_len % 256 == 0
        and piece_len * lax.axis_size("src") == target_len
    ):
        return fused(
            excitation, start, material, face_cell, face_count, face_weight, slot_panel,
            target_points, source_points,
        )
    slot_rank = jnp.arange(slot_count, dtype=jnp.int32) % capacity
    live_count = jnp.repeat(face_count.reshape(-1), capacity, total_repeat_length=slot_count)
    slot_scale = jnp.where(slot_rank < live_count, face_weight.reshape(-1), 0.0)
    compact = slot_count < piece_len
    vol_index = lax.axis_index("vol")
    src_index = lax.axis_index("src")
    src_count = lax.axis_size("src")
    panels = slot_panel.reshape(-1)
    if compact:
        own_points = jnp.concatenate(
            [
                jnp.take(lax.dynamic_slice_in_dim(source_points, vol_index * piece_len, piece_len, 1), panels, axis=1),
                jnp.take(lax.dynamic_slice_in_dim(target_points, src_index * piece_len, piece_len, 1), panels, axis=1),
                panels.astype(jnp.float32)[None],
            ]
        )
        own_targets = lax.dynamic_slice_in_dim(target_points, src_index * piece_len, piece_len, 1)
    else:
        owner_table = (
            panels[:, None] == jnp.arange(piece_len, dtype=jnp.int32)[None, :]
        ).astype(jnp.float32)
    flux_scale = float(P_SIZE) ** (-0.5)
    potential = start
    flux_own = jnp.zeros((exc_count, piece_len), jnp.float32)
    for outer_index in range(ITERS):
        current = with_rim(potential)
        nu_own = reluctivity(gradient_sq(pad_depth(current)), material)
        nu_ext = extended(nu_own, (("vol", 1), ("src", 2)), 1)
        weights = face_weights(nu_ext, domain_edges)
        diagonal = weights[0] + weights[1] + weights[2] + weights[3] + weights[4] + weights[5]
        cell_values = jnp.take(potential.reshape(exc_count, cell_count), slot_cells, axis=1)
        if compact:
            traces = (cell_values * slot_scale[None, :]).T
            message = traces if outer_index else jnp.concatenate([traces, own_points.T], axis=1)
            gathered = lax.all_gather(message, ("vol", "src"), axis=0, tiled=False)
            gathered = gathered.reshape(vol_count, src_count, slot_count, -1)
            if outer_index == 0:
                points = gathered[..., exc_count:]
                places = points[..., :3].reshape(-1, 3).T
                ids = points[..., 6]
                same = ids[..., :, None] == ids[..., None, :]
                rank = jnp.arange(slot_count)
                earlier = same & (rank[None, :] < rank[:, None])
                merge = (same & ~jnp.any(earlier, axis=-1)[..., None]).astype(jnp.float32)
                mine = lax.dynamic_index_in_dim(points, src_index, 1, keepdims=False)
                mine = mine.reshape(vol_count, vol_count, capacity, -1)
                mine = lax.dynamic_index_in_dim(mine, vol_index, 1, keepdims=False)
                slot_targets = mine[..., 3:6].reshape(-1, 3).T
                slot_kernel = kernel_block(slot_targets, places)
            arrived = gathered[..., :exc_count].reshape(
                vol_count, src_count, vol_count, capacity, exc_count
            )
            arrived = arrived.transpose(2, 1, 0, 3, 4).reshape(
                vol_count, src_count, slot_count, exc_count
            )
            density = jnp.einsum(
                "wsij,wsje->wsie", merge, arrived, precision=lax.Precision.HIGHEST
            )
            density = density.reshape(-1, exc_count).astype(jnp.bfloat16)
            returned = flux_scale * jnp.einsum(
                "tn,ne->te", slot_kernel, density, preferred_element_type=jnp.float32
            )
            if outer_index == ITERS - 1:
                flux_own = flux_scale * jnp.einsum(
                    "ne,tn->et",
                    density,
                    kernel_block(own_targets, places),
                    preferred_element_type=jnp.float32,
                )
        else:
            outgoing = (cell_values * slot_scale[None, :]).T.reshape(vol_count, capacity * exc_count)
            arrived = lax.all_to_all(outgoing, "vol", split_axis=0, concat_axis=0, tiled=True).reshape(
                slot_count, exc_count
            )
            density = jnp.dot(
                arrived.T,
                owner_table,
                precision=lax.Precision.HIGHEST,
                preferred_element_type=jnp.float32,
            ).astype(jnp.bfloat16)
            block_piece = lax.all_gather(density, "vol", axis=1, tiled=True)
            piece_count = block_piece.shape[1]
            step_len = 1024

            def one_step(step_index, partial_value):
                offset_index = step_index * step_len
                segment = lax.dynamic_slice_in_dim(block_piece, offset_index, step_len, 1)
                places = lax.dynamic_slice_in_dim(source_points, offset_index, step_len, 1)
                dist_sq = jnp.zeros((target_len, step_len), jnp.float32)
                for component in range(3):
                    offset = target_points[component][:, None] - places[component][None, :]
                    dist_sq = dist_sq + offset * offset
                kernel = lax.rsqrt(dist_sq + SOFTENING * SOFTENING).astype(jnp.bfloat16)
                return partial_value + jnp.einsum(
                    "en,tn->et", segment, kernel, preferred_element_type=jnp.float32
                )

            partial_flux = lax.fori_loop(
                0, piece_count // step_len, one_step, jnp.zeros((exc_count, target_len), jnp.float32)
            )
            flux_sum = lax.psum_scatter(partial_flux, "src", scatter_dimension=1, tiled=True)
            flux_own = flux_sum * flux_scale
            per_slot = jnp.dot(
                flux_own,
                owner_table.T,
                precision=lax.Precision.HIGHEST,
                preferred_element_type=jnp.float32,
            )
            returned = lax.all_to_all(
                per_slot.T.reshape(vol_count, capacity * exc_count),
                "vol",
                split_axis=0,
                concat_axis=0,
                tiled=True,
            ).reshape(slot_count, exc_count)
        contribution = returned.T * slot_scale[None, :]
        surface = (
            jnp.zeros((exc_count, cell_count), jnp.float32).at[:, slot_cells].add(contribution)
        )
        forcing = excitation + surface.reshape(excitation.shape)
        for sweep_index in range(SWEEPS):
            if sweep_index > 0:
                current = with_rim(potential)
            potential = relax(pad_depth(current), weights, diagonal, forcing)
    return (potential, flux_own)


def solution(mesh):
    return jax.shard_map(
        per_device,
        mesh=mesh,
        in_specs=(
            P(None, "vol", "src", None),
            P(None, "vol", "src", None),
            P("vol", "src", None),
            P("vol", "src", None),
            P("vol", "src", None),
            P("vol", "src", None),
            P("vol", "src", None),
            P(None, "vol"),
            P(None, "src"),
        ),
        out_specs=(P(None, "vol", "src", None), P(None, ("vol", "src"))),
        check_vma=False,
    )
```

```python
import functools

import jax
import jax.numpy as jnp
from jax import lax
from jax.experimental import pallas as pl
from jax.experimental.pallas import tpu as pltpu
from jax.sharding import PartitionSpec as P

P_SIZE = 65536
ITERS = 2
SWEEPS = 2


NU_BASE = (1.0, 0.05, 0.4)
NU_SATURATION = (0.0, 0.9, 0.3)
RELAXATION = 0.8
SOFTENING = 0.05


def extended(block, sides, width):
    for axis, dim in sides:
        count = lax.axis_size(axis)
        forward = [(i, i + 1) for i in range(count - 1)]
        backward = [(target, source) for source, target in forward]
        low = lax.ppermute(
            lax.slice_in_dim(block, block.shape[dim] - width, None, axis=dim), axis, forward
        )
        high = lax.ppermute(lax.slice_in_dim(block, 0, width, axis=dim), axis, backward)
        block = jnp.concatenate([low, block, high], axis=dim)
    return block


def reluctivity(grad_sq, material):
    base_value = jnp.zeros(material.shape, jnp.float32)
    slope_value = jnp.zeros(material.shape, jnp.float32)
    for material_id in range(3):
        picked = material == material_id
        base_value = jnp.where(picked, NU_BASE[material_id], base_value)
        slope_value = jnp.where(picked, NU_SATURATION[material_id], slope_value)
    return base_value[None] + slope_value[None] * grad_sq / (1.0 + grad_sq)


def gradient_sq(padded):
    along_x = 0.5 * (padded[:, 2:, 1:-1, 1:-1] - padded[:, :-2, 1:-1, 1:-1])
    along_y = 0.5 * (padded[:, 1:-1, 2:, 1:-1] - padded[:, 1:-1, :-2, 1:-1])
    along_z = 0.5 * (padded[:, 1:-1, 1:-1, 2:] - padded[:, 1:-1, 1:-1, :-2])
    return along_x * along_x + along_y * along_y + along_z * along_z


def pad_depth(values):
    return jnp.pad(values, ((0, 0), (0, 0), (0, 0), (1, 1)))


def face_weights(nu_ext, domain_edges):
    first_x, last_x, first_y, last_y = domain_edges
    interior = nu_ext[:, 1:-1, 1:-1]
    low_x = jnp.where(first_x, interior[:, :1], nu_ext[:, :1, 1:-1])
    high_x = jnp.where(last_x, interior[:, -1:], nu_ext[:, -1:, 1:-1])
    column = jnp.concatenate([low_x, interior, high_x], axis=1)
    low_y = jnp.where(first_y, interior[:, :, :1], nu_ext[:, 1:-1, :1])
    high_y = jnp.where(last_y, interior[:, :, -1:], nu_ext[:, 1:-1, -1:])
    row_ext = jnp.concatenate([low_y, interior, high_y], axis=2)
    depth_ext = jnp.pad(interior, ((0, 0), (0, 0), (0, 0), (1, 1)), mode="edge")
    return (
        0.5 * (interior + column[:, 2:]),
        0.5 * (interior + column[:, :-2]),
        0.5 * (interior + row_ext[:, :, 2:]),
        0.5 * (interior + row_ext[:, :, :-2]),
        0.5 * (interior + depth_ext[:, :, :, 2:]),
        0.5 * (interior + depth_ext[:, :, :, :-2]),
    )


def relax(padded, weights, diagonal, forcing):
    center = padded[:, 1:-1, 1:-1, 1:-1]
    neighbours = (
        padded[:, 2:, 1:-1, 1:-1],
        padded[:, :-2, 1:-1, 1:-1],
        padded[:, 1:-1, 2:, 1:-1],
        padded[:, 1:-1, :-2, 1:-1],
        padded[:, 1:-1, 1:-1, 2:],
        padded[:, 1:-1, 1:-1, :-2],
    )
    applied = diagonal * center
    for weight, neighbour in zip(weights, neighbours):
        applied = applied - weight * neighbour
    return center + RELAXATION * (forcing - applied) / diagonal


def kernel_block(targets, places):
    dist_sq = jnp.zeros((targets.shape[1], places.shape[1]), jnp.float32)
    for component in range(3):
        offset = targets[component][:, None] - places[component][None, :]
        dist_sq = dist_sq + offset * offset
    return lax.rsqrt(dist_sq + SOFTENING * SOFTENING).astype(jnp.bfloat16)


def with_rim(potential):
    return extended(potential, (("vol", 1), ("src", 2)), 1)


MESH = pl.DeviceIdType.MESH
LANES = 128
TILE = 8
NT = (((1,), (1,)), ((), ()))
NN = (((1,), (0,)), ((), ()))


def split_dot(values, selector, dims):
    total = None
    for _ in range(3):
        part = values.astype(jnp.bfloat16)
        term = lax.dot_general(part, selector, dims, preferred_element_type=jnp.float32)
        total = term if total is None else total + term
        values = values - part.astype(jnp.float32)
    return total


def one_hot(mask):
    return jnp.where(mask, 1.0, 0.0).astype(jnp.bfloat16)


def as_columns(rows):
    return jnp.concatenate([rows] * (LANES // rows.shape[0]), axis=0).T


def pair_kernel(columns, rows):
    dist_sq = None
    for column, row in zip(columns, rows):
        offset = column - row
        dist_sq = offset * offset if dist_sq is None else dist_sq + offset * offset
    return lax.rsqrt(dist_sq + SOFTENING * SOFTENING).astype(jnp.bfloat16)


def fused_kernel(
    vol_count, src_count, capacity, flux_scale,
    start_ref, exc_ref, mat_ref, cell_ref, live_ref, weight_ref, panel_ref, target_ref, source_ref,
    out_ref, flux_ref,
    pe, pf, nu, forcing, a_send, ax, ay, ac, b_send, bx, by, mat_near,
    tr_send, tr_recv, de_send, de_recv, ge_recv, ge_all, slot_kernel, dens_all,
    points_ref, geo_ref, ge_pair, ge_send, de_own, de_pair, gp_ss, gp_rs, dp_ss, dp_rs, halo_ss, halo_rs, tr_ss, tr_rs, de_ss, de_rs, ge_ss, ge_rs,
):
    width_x, width_y, exc_count, depth = start_ref.shape
    v, s = lax.axis_index("vol"), lax.axis_index("src")
    group = TILE // capacity
    slot_count = vol_count * capacity
    first_x, last_x = v == 0, v == vol_count - 1
    first_y, last_y = s == 0, s == src_count - 1

    def others(total, own, body):
        def step(index, carry):
            body(lax.rem(own + index, total))
            return carry

        lax.fori_loop(1, total, step, 0)

    barrier = pltpu.get_barrier_semaphore()

    def greet(v_other, s_other):
        pl.semaphore_signal(
            barrier, inc=1, device_id=(v_other, s_other), device_id_type=MESH
        )

    others(vol_count, v, lambda other: greet(other, s))
    others(src_count, s, lambda other: greet(v, other))
    near_x = jnp.where(first_x, 0, 1) + jnp.where(last_x, 0, 1)
    near_y = jnp.where(first_y, 0, 1) + jnp.where(last_y, 0, 1)
    for dv, in_x in ((1, jnp.logical_not(last_x)), (-1, jnp.logical_not(first_x))):
        for ds, in_y in ((1, jnp.logical_not(last_y)), (-1, jnp.logical_not(first_y))):
            pl.when(jnp.logical_and(in_x, in_y))(functools.partial(greet, v + dv, s + ds))

    lane = lax.broadcasted_iota(jnp.int32, (exc_count, depth), 1)
    at_low, at_high = lane == 0, lane == depth - 1
    row64 = lax.broadcasted_iota(jnp.int32, (slot_count, LANES), 0)
    lane64 = lax.broadcasted_iota(jnp.int32, (slot_count, LANES), 1)
    repeat_slots = one_hot(lane64 % slot_count == row64)

    def spread_rows(ref, selector):
        values = jnp.broadcast_to(ref[...].astype(jnp.float32), (TILE, ref.shape[1]))
        return split_dot(values, selector, NN)

    lane_row = lax.broadcasted_iota(jnp.int32, (1, LANES), 1)
    lane_owner = lax.broadcasted_iota(jnp.int32, (vol_count, LANES), 1) % slot_count // capacity
    pick_owner = one_hot(
        lane_owner == lax.broadcasted_iota(jnp.int32, (vol_count, LANES), 0)
    )
    slot_cell = spread_rows(cell_ref, repeat_slots)[0:1].astype(jnp.int32)
    slot_cell = jnp.where(lane_row < slot_count, slot_cell, -1)
    cell_row = slot_cell >> (depth.bit_length() - 1)
    cell_depth = jnp.where(slot_cell < 0, -1, slot_cell & (depth - 1))
    live = (lane_row % capacity).astype(jnp.float32) < spread_rows(live_ref, pick_owner)[0:1]
    slot_scale = jnp.where(
        live & (lane_row < slot_count), spread_rows(weight_ref, repeat_slots)[0:1], 0.0
    )
    pick_depth = one_hot(lax.broadcasted_iota(jnp.int32, (depth, LANES), 0) == cell_depth)
    chunk = 8

    def traces_of(read):
        total = jnp.zeros((exc_count, LANES), jnp.float32)
        for x in range(width_x):
            for y0 in range(0, width_y, chunk):
                block = read(x, y0).reshape(chunk * exc_count, depth)
                taken = split_dot(block, pick_depth, NN)
                for k in range(chunk):
                    row = x * width_y + y0 + k
                    total = total + jnp.where(
                        cell_row == row, taken[k * exc_count : (k + 1) * exc_count], 0.0
                    )
        total = total * slot_scale
        return as_columns(total)

    def joined(pieces):
        total = pieces[0]
        for k in range(1, src_count):
            total = total + pieces[k]
        return total

    def each_near(direction):
        dv, ds = direction
        sends, gets = True, True
        if dv > 0:
            sends, gets = jnp.logical_not(last_x), jnp.logical_not(first_x)
        elif dv < 0:
            sends, gets = jnp.logical_not(first_x), jnp.logical_not(last_x)
        if ds > 0:
            sends = jnp.logical_and(sends, jnp.logical_not(last_y))
            gets = jnp.logical_and(gets, jnp.logical_not(first_y))
        elif ds < 0:
            sends = jnp.logical_and(sends, jnp.logical_not(first_y))
            gets = jnp.logical_and(gets, jnp.logical_not(last_y))
        return sends, gets

    started = []

    def send_near(direction, src, dst, place):
        dv, ds = direction
        copy = pltpu.make_async_remote_copy(
            src_ref=src, dst_ref=dst, send_sem=halo_ss.at[place], recv_sem=halo_rs.at[place],
            device_id=(v + dv, s + ds), device_id_type=MESH,
        )
        sends, gets = each_near(direction)
        pl.when(sends)(copy.start)
        started.append((sends, copy))
        return gets, copy

    def land(gets, copy, put, zero):
        @pl.when(gets)
        def _():
            copy.wait_recv()
            put()

        pl.when(jnp.logical_not(gets))(zero)

    def land_into(pair, dst, src):
        def put():
            dst[...] = src[...].astype(dst.dtype)

        def zero():
            dst[...] = jnp.zeros(dst.shape, dst.dtype)

        land(pair[0], pair[1], put, zero)

    def pair_copy(src, dst, send_sems, recv_sems, other, owner):
        return pltpu.make_async_remote_copy(
            src_ref=src, dst_ref=dst.at[owner], send_sem=send_sems.at[other],
            recv_sem=recv_sems.at[owner], device_id=(v, other), device_id_type=MESH,
        )

    def geo_pair(other, owner):
        return pair_copy(geo_ref, ge_pair, gp_ss, gp_rs, other, owner)

    def density_pair(it, other, owner):
        return pair_copy(
            de_own.at[it], de_pair.at[it], dp_ss.at[it], dp_rs.at[it], other, owner
        )

    def geo_copy(other, owner):
        return pltpu.make_async_remote_copy(
            src_ref=ge_send, dst_ref=ge_recv.at[owner], send_sem=ge_ss.at[other],
            recv_sem=ge_rs.at[owner], device_id=(other, s), device_id_type=MESH,
        )

    def trace_copy(it, other, owner):
        tile = pl.multiple_of((other // group) * TILE, TILE)
        return pltpu.make_async_remote_copy(
            src_ref=tr_send.at[it, pl.ds(tile, TILE)], dst_ref=tr_recv.at[it, owner],
            send_sem=tr_ss.at[it, other], recv_sem=tr_rs.at[it, owner],
            device_id=(other, s), device_id_type=MESH,
        )

    def density_copy(it, other, owner):
        return pltpu.make_async_remote_copy(
            src_ref=de_send.at[it], dst_ref=de_recv.at[it, owner], send_sem=de_ss.at[it, other],
            recv_sem=de_rs.at[it, owner], device_id=(other, s), device_id_type=MESH,
        )

    def each_y(body):
        def some(index, carry):
            for k in range(4):
                body(index * 4 + k)
            return carry

        lax.fori_loop(0, width_y // 4, some, 0)

    def depth_near(block, low_fill, high_fill):
        up = jnp.where(at_high, high_fill, pltpu.roll(block, depth - 1, 1))
        down = jnp.where(at_low, low_fill, pltpu.roll(block, 1, 1))
        return up, down

    def nu_at(x, y, material):
        center = pe[x + 2, y + 2]
        up, down = depth_near(center, 0.0, 0.0)
        along_x = 0.5 * (pe[x + 3, y + 2] - pe[x + 1, y + 2])
        along_y = 0.5 * (pe[x + 2, y + 3] - pe[x + 2, y + 1])
        along_z = 0.5 * (up - down)
        grad_sq = along_x * along_x + along_y * along_y + along_z * along_z
        base = jnp.zeros(material.shape, jnp.float32)
        slope = jnp.zeros(material.shape, jnp.float32)
        for material_id in range(3):
            picked = material == material_id
            base = jnp.where(picked, NU_BASE[material_id], base)
            slope = jnp.where(picked, NU_SATURATION[material_id], slope)
        return base + slope * grad_sq / (1.0 + grad_sq)

    def all_nu():
        def one_y(y):
            own = []
            for x in range(width_x):
                value = nu_at(x, y, mat_ref[x, pl.ds(y, 1), :])
                nu[x + 1, y + 1] = value
                own.append(value)
            low = nu_at(-1, y, mat_near[0, width_x - 1, pl.ds(y, 1), :])
            high = nu_at(width_x, y, mat_near[1, 0, pl.ds(y, 1), :])
            nu[0, y + 1] = jnp.where(first_x, own[0], low)
            nu[width_x + 1, y + 1] = jnp.where(last_x, own[-1], high)

        each_y(one_y)
        for x in range(width_x):
            low = nu_at(x, -1, mat_near[2, x, width_y - 1 : width_y, :])
            high = nu_at(x, width_y, mat_near[3, x, 0:1, :])
            nu[x + 1, 0] = jnp.where(first_y, nu[x + 1, 1], low)
            nu[x + 1, width_y + 1] = jnp.where(last_y, nu[x + 1, width_y], high)

    def relaxed(read, x, y):
        own = nu[x + 1, y + 1]
        nu_up, nu_down = depth_near(own, own, own)
        center = read(x, y)
        up, down = depth_near(center, 0.0, 0.0)
        pairs = (
            (nu[x + 2, y + 1], read(x + 1, y)),
            (nu[x, y + 1], read(x - 1, y)),
            (nu[x + 1, y + 2], read(x, y + 1)),
            (nu[x + 1, y], read(x, y - 1)),
            (nu_up, up),
            (nu_down, down),
        )
        diagonal, pulled = None, None
        for near_nu, near in pairs:
            weight = 0.5 * (own + near_nu)
            diagonal = weight if diagonal is None else diagonal + weight
            pulled = weight * near if pulled is None else pulled + weight * near
        applied = diagonal * center - pulled
        return center + RELAXATION * (forcing[x, y] - applied) / diagonal

    def sweep(read, write):
        def one_y(y):
            for x in range(width_x):
                write(x, y, relaxed(read, x, y))

        each_y(one_y)

    def keep_start(y):
        for x in range(width_x):
            value = start_ref[x, y]
            pe[x + 2, y + 2] = value
            a_send[0, x, y] = value.astype(jnp.bfloat16)

    each_y(keep_start)

    def place_points():
        piece_len = points_ref.shape[1]
        points_ref[0:3, :] = source_ref[
            :, pl.ds(pl.multiple_of(v * piece_len, LANES), piece_len)
        ]
        points_ref[3:6, :] = target_ref[
            :, pl.ds(pl.multiple_of(s * piece_len, LANES), piece_len)
        ]
        points_ref[6:8, :] = jnp.zeros((2, piece_len), jnp.float32)
        lane_panel = spread_rows(panel_ref, repeat_slots)
        lane_index = lane_panel[0:1].astype(jnp.int32)
        total = jnp.zeros((TILE, LANES), jnp.float32)
        step = 256
        for k in range(0, piece_len, step):
            index = lax.broadcasted_iota(jnp.int32, (step, LANES), 0) + k
            total = total + split_dot(
                points_ref[:, k : k + step], one_hot(index == lane_index), NN
            )
        lane_live = lane_row // slot_count == s
        geo_ref[...] = jnp.where(lane_live, total, 0.0)
        row = lax.broadcasted_iota(jnp.int32, (LANES, LANES), 0)
        column = lax.broadcasted_iota(jnp.int32, (LANES, LANES), 1)
        earlier = (as_columns(lane_panel) == lane_panel[0:1]) & (row < column % slot_count)
        repeated = jnp.sum(jnp.where(earlier, 1.0, 0.0), axis=0, keepdims=True)
        arrival_slot = lane64 // TILE * capacity + lane64 % capacity
        row_panel = as_columns(spread_rows(panel_ref, one_hot(arrival_slot == row64)))
        keep = (row_panel == lane_panel[0:1]) & (repeated == 0.0) & lane_live
        return one_hot(keep & (row % TILE // capacity == lax.rem(v, group)))

    last_layer = pl.ds(width_x - 1, 1)
    per_iter = 12
    for it in range(ITERS):
        base_sem = it * per_iter
        tr_send[it] = traces_of(
            lambda x, y0: pe[x + 2, 2 + y0 : 2 + y0 + chunk]
        )
        tile = pl.multiple_of((v // group) * TILE, TILE)
        tr_recv[it, v] = tr_send[it, pl.ds(tile, TILE), :]
        if it == 0:
            pl.semaphore_wait(barrier, vol_count + src_count - 2 + near_x * near_y)
        others(vol_count, v, lambda other: trace_copy(it, other, v).start())
        if it == 0:
            near_mat = [
                send_near(direction, mat_ref, mat_near.at[k], ITERS * per_iter + k)
                for k, direction in enumerate(((1, 0), (-1, 0), (0, 1), (0, -1)))
            ]
        block = a_send.at[it]
        got_x = [
            send_near((1, 0), block.at[pl.ds(width_x - 2, 2)], ax.at[it, 0], base_sem),
            send_near((-1, 0), block.at[pl.ds(0, 2)], ax.at[it, 1], base_sem + 1),
        ]
        got_y = [
            send_near((0, 1), block.at[:, pl.ds(width_y - 2, 2)], ay.at[it, 0], base_sem + 2),
            send_near((0, -1), block.at[:, pl.ds(0, 2)], ay.at[it, 1], base_sem + 3),
        ]
        got_c = []
        for k, (dv, ds) in enumerate(((1, 1), (1, -1), (-1, 1), (-1, -1))):
            x = width_x - 1 if dv > 0 else 0
            y = width_y - 1 if ds > 0 else 0
            got_c.append(
                send_near((dv, ds), block.at[x, y], ac.at[it, k], base_sem + 4 + k)
            )

        if it == 0:
            merge = place_points()
            ge_pair[s] = geo_ref[...]
            others(src_count, s, lambda other: geo_pair(other, s).start())
            others(src_count, s, lambda other: geo_pair(other, other).wait_recv())
            ge_send[...] = joined(ge_pair[...])
            ge_recv[v] = ge_send[...]
            others(vol_count, v, lambda other: geo_copy(other, v).start())
        others(vol_count, v, lambda other: trace_copy(it, other, other).wait_recv())
        arrived = tr_recv[it].reshape(vol_count * TILE, LANES).T[:exc_count]
        density = split_dot(arrived, merge, NN).astype(jnp.bfloat16)
        de_own[it] = density
        de_pair[it, s] = density
        others(src_count, s, lambda other: density_pair(it, other, s).start())
        others(src_count, s, lambda other: density_pair(it, other, other).wait_recv())
        density = joined(de_pair[it].astype(jnp.float32)).astype(jnp.bfloat16)
        de_send[it] = density
        de_recv[it, v] = density
        others(vol_count, v, lambda other: density_copy(it, other, v).start())

        if it == 0:
            others(vol_count, v, lambda other: geo_copy(other, other).wait_recv())
            lanes = lax.broadcasted_iota(jnp.int32, (TILE, LANES), 1)
            mine = jnp.zeros((TILE, LANES), jnp.float32)
            for w in range(vol_count):
                piece = ge_recv[w]
                ge_all[:, w * LANES : (w + 1) * LANES] = piece
                shift = lax.rem(
                    w * capacity + 2 * LANES - s * slot_count - v * capacity, LANES
                )
                turned = pltpu.roll(piece, shift, 1)
                mine = mine + jnp.where(lanes // capacity == w, turned, 0.0)
            columns = as_columns(mine)
            columns = [columns[:, 3 + c : 4 + c] for c in range(3)]
            for w in range(vol_count):
                span = slice(w * LANES, (w + 1) * LANES)
                slot_kernel[:, span] = pair_kernel(
                    columns, [ge_all[c : c + 1, span] for c in range(3)]
                )

        others(vol_count, v, lambda other: density_copy(it, other, other).wait_recv())
        for w in range(vol_count):
            dens_all[:, w * LANES : (w + 1) * LANES] = de_recv[it, w]
        slot_flux = lax.dot_general(
            dens_all[...], slot_kernel[...], NT, preferred_element_type=jnp.float32
        )
        back = slot_flux * flux_scale * slot_scale
        for x in range(width_x):
            for y0 in range(0, width_y, chunk):
                spread = jnp.concatenate(
                    [
                        jnp.where(cell_row == x * width_y + y0 + k, back, 0.0)
                        for k in range(chunk)
                    ],
                    axis=0,
                )
                surface = split_dot(spread, pick_depth, NT)
                for k in range(chunk):
                    forcing[x, y0 + k] = (
                        exc_ref[x, y0 + k] + surface[k * exc_count : (k + 1) * exc_count]
                    )

        if it == 0:
            for k, pair in enumerate(near_mat):
                def zero(k=k):
                    mat_near[k] = jnp.zeros(mat_ref.shape, jnp.int32)

                land(pair[0], pair[1], lambda: None, zero)
        rows, cols = pl.ds(2, width_x), pl.ds(2, width_y)
        land_into(got_y[0], pe.at[rows, pl.ds(0, 2)], ay.at[it, 0])
        land_into(got_y[1], pe.at[rows, pl.ds(width_y + 2, 2)], ay.at[it, 1])
        for k, (dv, ds) in enumerate(((1, 1), (1, -1), (-1, 1), (-1, -1))):
            x = 1 if dv > 0 else width_x + 2
            y = 1 if ds > 0 else width_y + 2
            land_into(got_c[k], pe.at[x, y], ac.at[it, k])
        land_into(got_x[0], pe.at[pl.ds(0, 2), cols], ax.at[it, 0])
        land_into(got_x[1], pe.at[pl.ds(width_x + 2, 2), cols], ax.at[it, 1])
        all_nu()

        def write_first(x, y, value):
            pf[x + 1, y + 1] = value
            b_send[it, x, y] = value.astype(jnp.bfloat16)

        sweep(lambda x, y: pe[x + 2, y + 2], write_first)
        block = b_send.at[it]
        got_x = [
            send_near((1, 0), block.at[last_layer], bx.at[it, 0], base_sem + 8),
            send_near((-1, 0), block.at[pl.ds(0, 1)], bx.at[it, 1], base_sem + 9),
        ]
        got_y = [
            send_near((0, 1), block.at[:, pl.ds(width_y - 1, 1)], by.at[it, 0], base_sem + 10),
            send_near((0, -1), block.at[:, pl.ds(0, 1)], by.at[it, 1], base_sem + 11),
        ]
        if it == ITERS - 1:
            target_block = 256

            def one_block(index, carry):
                span = pl.ds(pl.multiple_of(index * target_block, target_block), target_block)
                points = jnp.concatenate(
                    [
                        as_columns(
                            points_ref[
                                :,
                                pl.ds(
                                    pl.multiple_of(index * target_block + k, LANES), LANES
                                ),
                            ]
                        )
                        for k in range(0, target_block, LANES)
                    ],
                    axis=0,
                )
                columns = [points[:, 3 + c : 4 + c] for c in range(3)]
                total = jnp.zeros((target_block, exc_count), jnp.float32)
                for k in range(0, vol_count * LANES, 2 * LANES):
                    part = slice(k, k + 2 * LANES)
                    tile = pair_kernel(columns, [ge_all[c : c + 1, part] for c in range(3)])
                    total = total + lax.dot_general(
                        tile, dens_all[:, part], NT, preferred_element_type=jnp.float32
                    )
                flux_ref[span, :] = total * flux_scale
                return carry

            lax.fori_loop(0, points_ref.shape[1] // target_block, one_block, 0)
        rows, cols = pl.ds(1, width_x), pl.ds(1, width_y)
        land_into(got_y[0], pf.at[rows, pl.ds(0, 1)], by.at[it, 0])
        land_into(got_y[1], pf.at[rows, pl.ds(width_y + 1, 1)], by.at[it, 1])
        land_into(got_x[0], pf.at[pl.ds(0, 1), cols], bx.at[it, 0])
        land_into(got_x[1], pf.at[pl.ds(width_x + 1, 1), cols], bx.at[it, 1])

        def write_second(x, y, value):
            if it == ITERS - 1:
                out_ref[x, y] = value
            else:
                pe[x + 2, y + 2] = value
                a_send[it + 1, x, y] = value.astype(jnp.bfloat16)

        sweep(lambda x, y: pf[x + 1, y + 1], write_second)

    for sends, copy in started:
        pl.when(sends)(copy.wait_send)
    others(src_count, s, lambda other: geo_pair(other, s).wait_send())
    others(vol_count, v, lambda other: geo_copy(other, v).wait_send())
    for it in range(ITERS):
        others(vol_count, v, lambda other: trace_copy(it, other, v).wait_send())
        others(src_count, s, lambda other: density_pair(it, other, s).wait_send())
        others(vol_count, v, lambda other: density_copy(it, other, v).wait_send())


def fused(
    excitation, start, material, face_cell, face_count, face_weight, slot_panel,
    target_points, source_points,
):
    vol_count, src_count = lax.axis_size("vol"), lax.axis_size("src")
    exc_count, width_x, width_y, depth = excitation.shape
    slot_count = face_cell.size
    capacity = slot_count // vol_count
    piece_len = source_points.shape[1] // vol_count
    vmem = pl.BlockSpec(memory_space=pltpu.VMEM)
    field = (width_x, width_y, exc_count, depth)
    plane = (exc_count, depth)
    f32, bf16 = jnp.float32, jnp.bfloat16
    halo_sems = ITERS * 12 + 4
    sources = vol_count * LANES
    dma = pltpu.SemaphoreType.DMA
    potential, flux = pl.pallas_call(
        functools.partial(
            fused_kernel, vol_count, src_count, capacity, float(P_SIZE) ** (-0.5)
        ),
        out_shape=(
            jax.ShapeDtypeStruct(field, f32),
            jax.ShapeDtypeStruct((piece_len, exc_count), f32),
        ),
        in_specs=[vmem] * 9,
        out_specs=(vmem, vmem),
        scratch_shapes=[
            pltpu.VMEM((width_x + 4, width_y + 4) + plane, f32),
            pltpu.VMEM((width_x + 2, width_y + 2) + plane, f32),
            pltpu.VMEM((width_x + 2, width_y + 2) + plane, f32),
            pltpu.VMEM(field, f32),
            pltpu.VMEM((ITERS,) + field, bf16),
            pltpu.VMEM((ITERS, 2, 2, width_y) + plane, bf16),
            pltpu.VMEM((ITERS, 2, width_x, 2) + plane, bf16),
            pltpu.VMEM((ITERS, 4) + plane, bf16),
            pltpu.VMEM((ITERS,) + field, bf16),
            pltpu.VMEM((ITERS, 2, 1, width_y) + plane, bf16),
            pltpu.VMEM((ITERS, 2, width_x, 1) + plane, bf16),
            pltpu.VMEM((4, width_x, width_y, depth), jnp.int32),
            pltpu.VMEM((ITERS, LANES, LANES), f32),
            pltpu.VMEM((ITERS, vol_count, TILE, LANES), f32),
            pltpu.VMEM((ITERS, exc_count, LANES), bf16),
            pltpu.VMEM((ITERS, vol_count, exc_count, LANES), bf16),
            pltpu.VMEM((vol_count, TILE, LANES), f32),
            pltpu.VMEM((TILE, sources), f32),
            pltpu.VMEM((LANES, sources), bf16),
            pltpu.VMEM((exc_count, sources), bf16),
            pltpu.VMEM((TILE, piece_len), f32),
            pltpu.VMEM((TILE, LANES), f32),
            pltpu.VMEM((src_count, TILE, LANES), f32),
            pltpu.VMEM((TILE, LANES), f32),
            pltpu.VMEM((ITERS, exc_count, LANES), bf16),
            pltpu.VMEM((ITERS, src_count, exc_count, LANES), bf16),
            dma((src_count,)),
            dma((src_count,)),
            dma((ITERS, src_count)),
            dma((ITERS, src_count)),
            dma((halo_sems,)),
            dma((halo_sems,)),
            dma((ITERS, vol_count)),
            dma((ITERS, vol_count)),
            dma((ITERS, vol_count)),
            dma((ITERS, vol_count)),
            dma((vol_count,)),
            dma((vol_count,)),
        ],
        compiler_params=pltpu.CompilerParams(
            collective_id=0, has_side_effects=True, vmem_limit_bytes=40 * 1024 * 1024
        ),
    )(
        start.transpose(1, 2, 0, 3),
        excitation.transpose(1, 2, 0, 3),
        material,
        face_cell.reshape(1, -1),
        face_count.reshape(1, -1),
        face_weight.reshape(1, -1),
        slot_panel.reshape(1, -1),
        target_points,
        source_points,
    )
    return potential.transpose(2, 0, 1, 3), flux.T


def per_device(
    excitation,
    start,
    material,
    face_cell,
    face_count,
    face_weight,
    slot_panel,
    target_points,
    source_points,
):
    vol_count = lax.axis_size("vol")
    first_x = lax.axis_index("vol") == 0
    last_x = lax.axis_index("vol") == vol_count - 1
    first_y = lax.axis_index("src") == 0
    last_y = lax.axis_index("src") == lax.axis_size("src") - 1
    domain_edges = (first_x, last_x, first_y, last_y)
    exc_count, width_x, width_y, depth_len = excitation.shape
    cell_count = width_x * width_y * depth_len
    slot_cells = face_cell.reshape(-1)
    slot_count = slot_cells.shape[0]
    capacity = slot_count // vol_count
    piece_len = source_points.shape[1] // vol_count
    target_len = target_points.shape[1]
    lane_tile = LANES == depth_len == slot_count * lax.axis_size("src")
    if (
        lane_tile
        and vol_count * TILE == LANES
        and TILE % capacity == 0
        and LANES % exc_count == 0
        and exc_count % 16 == 0
        and width_x >= 2
        and width_y % 8 == 0
        and piece_len % 256 == 0
        and piece_len * lax.axis_size("src") == target_len
    ):
        return fused(
            excitation, start, material, face_cell, face_count, face_weight, slot_panel,
            target_points, source_points,
        )
    slot_rank = jnp.arange(slot_count, dtype=jnp.int32) % capacity
    live_count = jnp.repeat(face_count.reshape(-1), capacity, total_repeat_length=slot_count)
    slot_scale = jnp.where(slot_rank < live_count, face_weight.reshape(-1), 0.0)
    compact = slot_count < piece_len
    vol_index = lax.axis_index("vol")
    src_index = lax.axis_index("src")
    src_count = lax.axis_size("src")
    panels = slot_panel.reshape(-1)
    if compact:
        own_points = jnp.concatenate(
            [
                jnp.take(lax.dynamic_slice_in_dim(source_points, vol_index * piece_len, piece_len, 1), panels, axis=1),
                jnp.take(lax.dynamic_slice_in_dim(target_points, src_index * piece_len, piece_len, 1), panels, axis=1),
                panels.astype(jnp.float32)[None],
            ]
        )
        own_targets = lax.dynamic_slice_in_dim(target_points, src_index * piece_len, piece_len, 1)
    else:
        owner_table = (
            panels[:, None] == jnp.arange(piece_len, dtype=jnp.int32)[None, :]
        ).astype(jnp.float32)
    flux_scale = float(P_SIZE) ** (-0.5)
    potential = start
    flux_own = jnp.zeros((exc_count, piece_len), jnp.float32)
    for outer_index in range(ITERS):
        current = with_rim(potential)
        nu_own = reluctivity(gradient_sq(pad_depth(current)), material)
        nu_ext = extended(nu_own, (("vol", 1), ("src", 2)), 1)
        weights = face_weights(nu_ext, domain_edges)
        diagonal = weights[0] + weights[1] + weights[2] + weights[3] + weights[4] + weights[5]
        cell_values = jnp.take(potential.reshape(exc_count, cell_count), slot_cells, axis=1)
        if compact:
            traces = (cell_values * slot_scale[None, :]).T
            message = traces if outer_index else jnp.concatenate([traces, own_points.T], axis=1)
            gathered = lax.all_gather(message, ("vol", "src"), axis=0, tiled=False)
            gathered = gathered.reshape(vol_count, src_count, slot_count, -1)
            if outer_index == 0:
                points = gathered[..., exc_count:]
                places = points[..., :3].reshape(-1, 3).T
                ids = points[..., 6]
                same = ids[..., :, None] == ids[..., None, :]
                rank = jnp.arange(slot_count)
                earlier = same & (rank[None, :] < rank[:, None])
                merge = (same & ~jnp.any(earlier, axis=-1)[..., None]).astype(jnp.float32)
                mine = lax.dynamic_index_in_dim(points, src_index, 1, keepdims=False)
                mine = mine.reshape(vol_count, vol_count, capacity, -1)
                mine = lax.dynamic_index_in_dim(mine, vol_index, 1, keepdims=False)
                slot_targets = mine[..., 3:6].reshape(-1, 3).T
                slot_kernel = kernel_block(slot_targets, places)
            arrived = gathered[..., :exc_count].reshape(
                vol_count, src_count, vol_count, capacity, exc_count
            )
            arrived = arrived.transpose(2, 1, 0, 3, 4).reshape(
                vol_count, src_count, slot_count, exc_count
            )
            density = jnp.einsum(
                "wsij,wsje->wsie", merge, arrived, precision=lax.Precision.HIGHEST
            )
            density = density.reshape(-1, exc_count).astype(jnp.bfloat16)
            returned = flux_scale * jnp.einsum(
                "tn,ne->te", slot_kernel, density, preferred_element_type=jnp.float32
            )
            if outer_index == ITERS - 1:
                flux_own = flux_scale * jnp.einsum(
                    "ne,tn->et",
                    density,
                    kernel_block(own_targets, places),
                    preferred_element_type=jnp.float32,
                )
        else:
            outgoing = (cell_values * slot_scale[None, :]).T.reshape(vol_count, capacity * exc_count)
            arrived = lax.all_to_all(outgoing, "vol", split_axis=0, concat_axis=0, tiled=True).reshape(
                slot_count, exc_count
            )
            density = jnp.dot(
                arrived.T,
                owner_table,
                precision=lax.Precision.HIGHEST,
                preferred_element_type=jnp.float32,
            ).astype(jnp.bfloat16)
            block_piece = lax.all_gather(density, "vol", axis=1, tiled=True)
            piece_count = block_piece.shape[1]
            step_len = 1024

            def one_step(step_index, partial_value):
                offset_index = step_index * step_len
                segment = lax.dynamic_slice_in_dim(block_piece, offset_index, step_len, 1)
                places = lax.dynamic_slice_in_dim(source_points, offset_index, step_len, 1)
                dist_sq = jnp.zeros((target_len, step_len), jnp.float32)
                for component in range(3):
                    offset = target_points[component][:, None] - places[component][None, :]
                    dist_sq = dist_sq + offset * offset
                kernel = lax.rsqrt(dist_sq + SOFTENING * SOFTENING).astype(jnp.bfloat16)
                return partial_value + jnp.einsum(
                    "en,tn->et", segment, kernel, preferred_element_type=jnp.float32
                )

            partial_flux = lax.fori_loop(
                0, piece_count // step_len, one_step, jnp.zeros((exc_count, target_len), jnp.float32)
            )
            flux_sum = lax.psum_scatter(partial_flux, "src", scatter_dimension=1, tiled=True)
            flux_own = flux_sum * flux_scale
            per_slot = jnp.dot(
                flux_own,
                owner_table.T,
                precision=lax.Precision.HIGHEST,
                preferred_element_type=jnp.float32,
            )
            returned = lax.all_to_all(
                per_slot.T.reshape(vol_count, capacity * exc_count),
                "vol",
                split_axis=0,
                concat_axis=0,
                tiled=True,
            ).reshape(slot_count, exc_count)
        contribution = returned.T * slot_scale[None, :]
        surface = (
            jnp.zeros((exc_count, cell_count), jnp.float32).at[:, slot_cells].add(contribution)
        )
        forcing = excitation + surface.reshape(excitation.shape)
        for sweep_index in range(SWEEPS):
            if sweep_index > 0:
                current = with_rim(potential)
            potential = relax(pad_depth(current), weights, diagonal, forcing)
    return (potential, flux_own)


def solution(mesh):
    return jax.shard_map(
        per_device,
        mesh=mesh,
        in_specs=(
            P(None, "vol", "src", None),
            P(None, "vol", "src", None),
            P("vol", "src", None),
            P("vol", "src", None),
            P("vol", "src", None),
            P("vol", "src", None),
            P("vol", "src", None),
            P(None, "vol"),
            P(None, "src"),
        ),
        out_specs=(P(None, "vol", "src", None), P(None, ("vol", "src"))),
        check_vma=False,
    )
```

```python
import functools

import jax
import jax.numpy as jnp
from jax import lax
from jax.experimental import pallas as pl
from jax.experimental.pallas import tpu as pltpu
from jax.sharding import PartitionSpec as P

P_SIZE = 65536
ITERS = 2
SWEEPS = 2


NU_BASE = (1.0, 0.05, 0.4)
NU_SATURATION = (0.0, 0.9, 0.3)
RELAXATION = 0.8
SOFTENING = 0.05


def extended(block, sides, width):
    for axis, dim in sides:
        count = lax.axis_size(axis)
        forward = [(i, i + 1) for i in range(count - 1)]
        backward = [(target, source) for source, target in forward]
        low = lax.ppermute(
            lax.slice_in_dim(block, block.shape[dim] - width, None, axis=dim), axis, forward
        )
        high = lax.ppermute(lax.slice_in_dim(block, 0, width, axis=dim), axis, backward)
        block = jnp.concatenate([low, block, high], axis=dim)
    return block


def reluctivity(grad_sq, material):
    base_value = jnp.zeros(material.shape, jnp.float32)
    slope_value = jnp.zeros(material.shape, jnp.float32)
    for material_id in range(3):
        picked = material == material_id
        base_value = jnp.where(picked, NU_BASE[material_id], base_value)
        slope_value = jnp.where(picked, NU_SATURATION[material_id], slope_value)
    return base_value[None] + slope_value[None] * grad_sq / (1.0 + grad_sq)


def gradient_sq(padded):
    along_x = 0.5 * (padded[:, 2:, 1:-1, 1:-1] - padded[:, :-2, 1:-1, 1:-1])
    along_y = 0.5 * (padded[:, 1:-1, 2:, 1:-1] - padded[:, 1:-1, :-2, 1:-1])
    along_z = 0.5 * (padded[:, 1:-1, 1:-1, 2:] - padded[:, 1:-1, 1:-1, :-2])
    return along_x * along_x + along_y * along_y + along_z * along_z


def pad_depth(values):
    return jnp.pad(values, ((0, 0), (0, 0), (0, 0), (1, 1)))


def face_weights(nu_ext, domain_edges):
    first_x, last_x, first_y, last_y = domain_edges
    interior = nu_ext[:, 1:-1, 1:-1]
    low_x = jnp.where(first_x, interior[:, :1], nu_ext[:, :1, 1:-1])
    high_x = jnp.where(last_x, interior[:, -1:], nu_ext[:, -1:, 1:-1])
    column = jnp.concatenate([low_x, interior, high_x], axis=1)
    low_y = jnp.where(first_y, interior[:, :, :1], nu_ext[:, 1:-1, :1])
    high_y = jnp.where(last_y, interior[:, :, -1:], nu_ext[:, 1:-1, -1:])
    row_ext = jnp.concatenate([low_y, interior, high_y], axis=2)
    depth_ext = jnp.pad(interior, ((0, 0), (0, 0), (0, 0), (1, 1)), mode="edge")
    return (
        0.5 * (interior + column[:, 2:]),
        0.5 * (interior + column[:, :-2]),
        0.5 * (interior + row_ext[:, :, 2:]),
        0.5 * (interior + row_ext[:, :, :-2]),
        0.5 * (interior + depth_ext[:, :, :, 2:]),
        0.5 * (interior + depth_ext[:, :, :, :-2]),
    )


def relax(padded, weights, diagonal, forcing):
    center = padded[:, 1:-1, 1:-1, 1:-1]
    neighbours = (
        padded[:, 2:, 1:-1, 1:-1],
        padded[:, :-2, 1:-1, 1:-1],
        padded[:, 1:-1, 2:, 1:-1],
        padded[:, 1:-1, :-2, 1:-1],
        padded[:, 1:-1, 1:-1, 2:],
        padded[:, 1:-1, 1:-1, :-2],
    )
    applied = diagonal * center
    for weight, neighbour in zip(weights, neighbours):
        applied = applied - weight * neighbour
    return center + RELAXATION * (forcing - applied) / diagonal


def kernel_block(targets, places):
    dist_sq = jnp.zeros((targets.shape[1], places.shape[1]), jnp.float32)
    for component in range(3):
        offset = targets[component][:, None] - places[component][None, :]
        dist_sq = dist_sq + offset * offset
    return lax.rsqrt(dist_sq + SOFTENING * SOFTENING).astype(jnp.bfloat16)


def with_rim(potential):
    return extended(potential, (("vol", 1), ("src", 2)), 1)


MESH = pl.DeviceIdType.MESH
LANES = 128
TILE = 8
NT = (((1,), (1,)), ((), ()))
NN = (((1,), (0,)), ((), ()))


def split_dot(values, selector, dims):
    total = None
    for _ in range(3):
        part = values.astype(jnp.bfloat16)
        term = lax.dot_general(part, selector, dims, preferred_element_type=jnp.float32)
        total = term if total is None else total + term
        values = values - part.astype(jnp.float32)
    return total


def one_hot(mask):
    return jnp.where(mask, 1.0, 0.0).astype(jnp.bfloat16)


def as_columns(rows):
    return jnp.concatenate([rows] * (LANES // rows.shape[0]), axis=0).T


def pair_kernel(columns, rows):
    dist_sq = None
    for column, row in zip(columns, rows):
        offset = column - row
        dist_sq = offset * offset if dist_sq is None else dist_sq + offset * offset
    return lax.rsqrt(dist_sq + SOFTENING * SOFTENING).astype(jnp.bfloat16)


def fused_kernel(
    vol_count, src_count, capacity, flux_scale,
    start_ref, exc_ref, mat_ref, cell_ref, live_ref, weight_ref, panel_ref, target_ref, source_ref,
    out_ref, flux_ref,
    pe, pf, nu, forcing, a_send, ax, ay, ac, b_send, bx, by, mat_near,
    tr_send, tr_recv, de_send, de_recv, ge_recv, ge_all, slot_kernel, dens_all,
    points_ref, geo_ref, ge_pair, ge_send, de_own, de_pair, gp_ss, gp_rs, dp_ss, dp_rs, halo_ss, halo_rs, tr_ss, tr_rs, de_ss, de_rs, ge_ss, ge_rs,
):
    width_x, width_y, exc_count, depth = start_ref.shape
    v, s = lax.axis_index("vol"), lax.axis_index("src")
    group = TILE // capacity
    slot_count = vol_count * capacity
    first_x, last_x = v == 0, v == vol_count - 1
    first_y, last_y = s == 0, s == src_count - 1

    def others(total, own, body):
        def step(index, carry):
            body(lax.rem(own + index, total))
            return carry

        lax.fori_loop(1, total, step, 0)

    barrier = pltpu.get_barrier_semaphore()

    def greet(v_other, s_other):
        pl.semaphore_signal(
            barrier, inc=1, device_id=(v_other, s_other), device_id_type=MESH
        )

    others(vol_count, v, lambda other: greet(other, s))
    others(src_count, s, lambda other: greet(v, other))
    near_x = jnp.where(first_x, 0, 1) + jnp.where(last_x, 0, 1)
    near_y = jnp.where(first_y, 0, 1) + jnp.where(last_y, 0, 1)
    for dv, in_x in ((1, jnp.logical_not(last_x)), (-1, jnp.logical_not(first_x))):
        for ds, in_y in ((1, jnp.logical_not(last_y)), (-1, jnp.logical_not(first_y))):
            pl.when(jnp.logical_and(in_x, in_y))(functools.partial(greet, v + dv, s + ds))

    lane = lax.broadcasted_iota(jnp.int32, (exc_count, depth), 1)
    at_low, at_high = lane == 0, lane == depth - 1
    row64 = lax.broadcasted_iota(jnp.int32, (slot_count, LANES), 0)
    lane64 = lax.broadcasted_iota(jnp.int32, (slot_count, LANES), 1)
    repeat_slots = one_hot(lane64 % slot_count == row64)

    def spread_rows(ref, selector):
        values = jnp.broadcast_to(ref[...].astype(jnp.float32), (TILE, ref.shape[1]))
        return split_dot(values, selector, NN)

    lane_row = lax.broadcasted_iota(jnp.int32, (1, LANES), 1)
    lane_owner = lax.broadcasted_iota(jnp.int32, (vol_count, LANES), 1) % slot_count // capacity
    pick_owner = one_hot(
        lane_owner == lax.broadcasted_iota(jnp.int32, (vol_count, LANES), 0)
    )
    slot_cell = spread_rows(cell_ref, repeat_slots)[0:1].astype(jnp.int32)
    slot_cell = jnp.where(lane_row < slot_count, slot_cell, -1)
    cell_row = slot_cell >> (depth.bit_length() - 1)
    cell_depth = jnp.where(slot_cell < 0, -1, slot_cell & (depth - 1))
    live = (lane_row % capacity).astype(jnp.float32) < spread_rows(live_ref, pick_owner)[0:1]
    slot_scale = jnp.where(
        live & (lane_row < slot_count), spread_rows(weight_ref, repeat_slots)[0:1], 0.0
    )
    pick_depth = one_hot(lax.broadcasted_iota(jnp.int32, (depth, LANES), 0) == cell_depth)
    chunk = 8

    def traces_of(read):
        total = jnp.zeros((exc_count, LANES), jnp.float32)
        for x in range(width_x):
            for y0 in range(0, width_y, chunk):
                block = read(x, y0).reshape(chunk * exc_count, depth)
                taken = split_dot(block, pick_depth, NN)
                for k in range(chunk):
                    row = x * width_y + y0 + k
                    total = total + jnp.where(
                        cell_row == row, taken[k * exc_count : (k + 1) * exc_count], 0.0
                    )
        total = total * slot_scale
        return as_columns(total)

    def joined(pieces):
        total = pieces[0]
        for k in range(1, src_count):
            total = total + pieces[k]
        return total

    def each_near(direction):
        dv, ds = direction
        sends, gets = True, True
        if dv > 0:
            sends, gets = jnp.logical_not(last_x), jnp.logical_not(first_x)
        elif dv < 0:
            sends, gets = jnp.logical_not(first_x), jnp.logical_not(last_x)
        if ds > 0:
            sends = jnp.logical_and(sends, jnp.logical_not(last_y))
            gets = jnp.logical_and(gets, jnp.logical_not(first_y))
        elif ds < 0:
            sends = jnp.logical_and(sends, jnp.logical_not(first_y))
            gets = jnp.logical_and(gets, jnp.logical_not(last_y))
        return sends, gets

    started = []

    def send_near(direction, src, dst, place):
        dv, ds = direction
        copy = pltpu.make_async_remote_copy(
            src_ref=src, dst_ref=dst, send_sem=halo_ss.at[place], recv_sem=halo_rs.at[place],
            device_id=(v + dv, s + ds), device_id_type=MESH,
        )
        sends, gets = each_near(direction)
        pl.when(sends)(copy.start)
        started.append((sends, copy))
        return gets, copy

    def land(gets, copy, put, zero):
        @pl.when(gets)
        def _():
            copy.wait_recv()
            put()

        pl.when(jnp.logical_not(gets))(zero)

    def land_into(pair, dst, src):
        def put():
            dst[...] = src[...].astype(dst.dtype)

        def zero():
            dst[...] = jnp.zeros(dst.shape, dst.dtype)

        land(pair[0], pair[1], put, zero)

    def pair_copy(src, dst, send_sems, recv_sems, other, owner):
        return pltpu.make_async_remote_copy(
            src_ref=src, dst_ref=dst.at[owner], send_sem=send_sems.at[other],
            recv_sem=recv_sems.at[owner], device_id=(v, other), device_id_type=MESH,
        )

    def geo_pair(other, owner):
        return pair_copy(geo_ref, ge_pair, gp_ss, gp_rs, other, owner)

    def density_pair(it, other, owner):
        return pair_copy(
            de_own.at[it], de_pair.at[it], dp_ss.at[it], dp_rs.at[it], other, owner
        )

    def geo_copy(other, owner):
        return pltpu.make_async_remote_copy(
            src_ref=ge_send, dst_ref=ge_recv.at[owner], send_sem=ge_ss.at[other],
            recv_sem=ge_rs.at[owner], device_id=(other, s), device_id_type=MESH,
        )

    def trace_copy(it, other, owner):
        tile = pl.multiple_of((other // group) * TILE, TILE)
        return pltpu.make_async_remote_copy(
            src_ref=tr_send.at[it, pl.ds(tile, TILE)], dst_ref=tr_recv.at[it, owner],
            send_sem=tr_ss.at[it, other], recv_sem=tr_rs.at[it, owner],
            device_id=(other, s), device_id_type=MESH,
        )

    def density_copy(it, other, owner):
        return pltpu.make_async_remote_copy(
            src_ref=de_send.at[it], dst_ref=de_recv.at[it, owner], send_sem=de_ss.at[it, other],
            recv_sem=de_rs.at[it, owner], device_id=(other, s), device_id_type=MESH,
        )

    chunk_rows = 4
    chunk_count = width_y // chunk_rows

    def chunk_y(part, body):
        for k in range(chunk_rows):
            body(part * chunk_rows + k)

    def each_y(body):
        def some(index, carry):
            for k in range(4):
                body(index * 4 + k)
            return carry

        lax.fori_loop(0, width_y // 4, some, 0)

    def depth_near(block, low_fill, high_fill):
        up = jnp.where(at_high, high_fill, pltpu.roll(block, depth - 1, 1))
        down = jnp.where(at_low, low_fill, pltpu.roll(block, 1, 1))
        return up, down

    def nu_at(x, y, material):
        center = pe[x + 2, y + 2]
        up, down = depth_near(center, 0.0, 0.0)
        along_x = 0.5 * (pe[x + 3, y + 2] - pe[x + 1, y + 2])
        along_y = 0.5 * (pe[x + 2, y + 3] - pe[x + 2, y + 1])
        along_z = 0.5 * (up - down)
        grad_sq = along_x * along_x + along_y * along_y + along_z * along_z
        base = jnp.zeros(material.shape, jnp.float32)
        slope = jnp.zeros(material.shape, jnp.float32)
        for material_id in range(3):
            picked = material == material_id
            base = jnp.where(picked, NU_BASE[material_id], base)
            slope = jnp.where(picked, NU_SATURATION[material_id], slope)
        return base + slope * grad_sq / (1.0 + grad_sq)

    def nu_chunk(part):
        def one_y(y):
            own = []
            for x in range(width_x):
                value = nu_at(x, y, mat_ref[x, y : y + 1, :])
                nu[x + 1, y + 1] = value
                own.append(value)
            low = nu_at(-1, y, mat_near[0, width_x - 1, y : y + 1, :])
            high = nu_at(width_x, y, mat_near[1, 0, y : y + 1, :])
            nu[0, y + 1] = jnp.where(first_x, own[0], low)
            nu[width_x + 1, y + 1] = jnp.where(last_x, own[-1], high)

        chunk_y(part, one_y)
        for x in range(width_x):
            if part == 0:
                low = nu_at(x, -1, mat_near[2, x, width_y - 1 : width_y, :])
                nu[x + 1, 0] = jnp.where(first_y, nu[x + 1, 1], low)
            if part == chunk_count - 1:
                high = nu_at(x, width_y, mat_near[3, x, 0:1, :])
                nu[x + 1, width_y + 1] = jnp.where(last_y, nu[x + 1, width_y], high)

    def relaxed(read, x, y):
        own = nu[x + 1, y + 1]
        nu_up, nu_down = depth_near(own, own, own)
        center = read(x, y)
        up, down = depth_near(center, 0.0, 0.0)
        pairs = (
            (nu[x + 2, y + 1], read(x + 1, y)),
            (nu[x, y + 1], read(x - 1, y)),
            (nu[x + 1, y + 2], read(x, y + 1)),
            (nu[x + 1, y], read(x, y - 1)),
            (nu_up, up),
            (nu_down, down),
        )
        diagonal, pulled = None, None
        for near_nu, near in pairs:
            weight = 0.5 * (own + near_nu)
            diagonal = weight if diagonal is None else diagonal + weight
            pulled = weight * near if pulled is None else pulled + weight * near
        applied = diagonal * center - pulled
        return center + RELAXATION * (forcing[x, y] - applied) / diagonal

    def sweep(part, read, write):
        def one_y(y):
            for x in range(width_x):
                write(x, y, relaxed(read, x, y))

        chunk_y(part, one_y)

    def keep_start(y):
        for x in range(width_x):
            value = start_ref[x, y]
            pe[x + 2, y + 2] = value
            a_send[0, x, y] = value.astype(jnp.bfloat16)

    each_y(keep_start)

    def place_points():
        piece_len = points_ref.shape[1]
        points_ref[0:3, :] = source_ref[
            :, pl.ds(pl.multiple_of(v * piece_len, LANES), piece_len)
        ]
        points_ref[3:6, :] = target_ref[
            :, pl.ds(pl.multiple_of(s * piece_len, LANES), piece_len)
        ]
        points_ref[6:8, :] = jnp.zeros((2, piece_len), jnp.float32)
        lane_panel = spread_rows(panel_ref, repeat_slots)
        lane_index = lane_panel[0:1].astype(jnp.int32)
        total = jnp.zeros((TILE, LANES), jnp.float32)
        step = 256
        for k in range(0, piece_len, step):
            index = lax.broadcasted_iota(jnp.int32, (step, LANES), 0) + k
            total = total + split_dot(
                points_ref[:, k : k + step], one_hot(index == lane_index), NN
            )
        lane_live = lane_row // slot_count == s
        geo_ref[...] = jnp.where(lane_live, total, 0.0)
        row = lax.broadcasted_iota(jnp.int32, (LANES, LANES), 0)
        column = lax.broadcasted_iota(jnp.int32, (LANES, LANES), 1)
        earlier = (as_columns(lane_panel) == lane_panel[0:1]) & (row < column % slot_count)
        repeated = jnp.sum(jnp.where(earlier, 1.0, 0.0), axis=0, keepdims=True)
        arrival_slot = lane64 // TILE * capacity + lane64 % capacity
        row_panel = as_columns(spread_rows(panel_ref, one_hot(arrival_slot == row64)))
        keep = (row_panel == lane_panel[0:1]) & (repeated == 0.0) & lane_live
        return one_hot(keep & (row % TILE // capacity == lax.rem(v, group)))

    last_layer = pl.ds(width_x - 1, 1)
    per_iter = 8 + width_y
    for it in range(ITERS):
        base_sem = it * per_iter
        tr_send[it] = traces_of(
            lambda x, y0: pe[x + 2, 2 + y0 : 2 + y0 + chunk]
        )
        tile = pl.multiple_of((v // group) * TILE, TILE)
        tr_recv[it, v] = tr_send[it, pl.ds(tile, TILE), :]
        if it == 0:
            pl.semaphore_wait(barrier, vol_count + src_count - 2 + near_x * near_y)
        others(vol_count, v, lambda other: trace_copy(it, other, v).start())
        if it == 0:
            near_mat = [
                send_near(direction, mat_ref, mat_near.at[k], ITERS * per_iter + k)
                for k, direction in enumerate(((1, 0), (-1, 0), (0, 1), (0, -1)))
            ]
        block = a_send.at[it]
        got_x = []
        for part in range(chunk_count):
            span = pl.ds(part * chunk_rows, chunk_rows)
            place = base_sem + 8 + 2 * part
            got_x.append(
                (
                    send_near(
                        (1, 0), block.at[pl.ds(width_x - 2, 2), span],
                        ax.at[it, 0, :, span], place,
                    ),
                    send_near(
                        (-1, 0), block.at[pl.ds(0, 2), span], ax.at[it, 1, :, span], place + 1
                    ),
                )
            )
        got_y = [
            send_near((0, 1), block.at[:, pl.ds(width_y - 2, 2)], ay.at[it, 0], base_sem),
            send_near((0, -1), block.at[:, pl.ds(0, 2)], ay.at[it, 1], base_sem + 1),
        ]
        got_c = []
        for k, (dv, ds) in enumerate(((1, 1), (1, -1), (-1, 1), (-1, -1))):
            x = width_x - 1 if dv > 0 else 0
            y = width_y - 1 if ds > 0 else 0
            got_c.append(
                send_near((dv, ds), block.at[x, y], ac.at[it, k], base_sem + 2 + k)
            )

        if it == 0:
            merge = place_points()
            ge_pair[s] = geo_ref[...]
            others(src_count, s, lambda other: geo_pair(other, s).start())
            others(src_count, s, lambda other: geo_pair(other, other).wait_recv())
            ge_send[...] = joined(ge_pair[...])
            ge_recv[v] = ge_send[...]
            others(vol_count, v, lambda other: geo_copy(other, v).start())
        others(vol_count, v, lambda other: trace_copy(it, other, other).wait_recv())
        arrived = tr_recv[it].reshape(vol_count * TILE, LANES).T[:exc_count]
        density = split_dot(arrived, merge, NN).astype(jnp.bfloat16)
        de_own[it] = density
        de_pair[it, s] = density
        others(src_count, s, lambda other: density_pair(it, other, s).start())
        others(src_count, s, lambda other: density_pair(it, other, other).wait_recv())
        density = joined(de_pair[it].astype(jnp.float32)).astype(jnp.bfloat16)
        de_send[it] = density
        de_recv[it, v] = density
        others(vol_count, v, lambda other: density_copy(it, other, v).start())

        if it == 0:
            others(vol_count, v, lambda other: geo_copy(other, other).wait_recv())
            lanes = lax.broadcasted_iota(jnp.int32, (TILE, LANES), 1)
            mine = jnp.zeros((TILE, LANES), jnp.float32)
            for w in range(vol_count):
                piece = ge_recv[w]
                ge_all[:, w * LANES : (w + 1) * LANES] = piece
                shift = lax.rem(
                    w * capacity + 2 * LANES - s * slot_count - v * capacity, LANES
                )
                turned = pltpu.roll(piece, shift, 1)
                mine = mine + jnp.where(lanes // capacity == w, turned, 0.0)
            columns = as_columns(mine)
            columns = [columns[:, 3 + c : 4 + c] for c in range(3)]
            for w in range(vol_count):
                span = slice(w * LANES, (w + 1) * LANES)
                slot_kernel[:, span] = pair_kernel(
                    columns, [ge_all[c : c + 1, span] for c in range(3)]
                )

        others(vol_count, v, lambda other: density_copy(it, other, other).wait_recv())
        for w in range(vol_count):
            dens_all[:, w * LANES : (w + 1) * LANES] = de_recv[it, w]
        slot_flux = lax.dot_general(
            dens_all[...], slot_kernel[...], NT, preferred_element_type=jnp.float32
        )
        back = slot_flux * flux_scale * slot_scale
        for x in range(width_x):
            for y0 in range(0, width_y, chunk):
                spread = jnp.concatenate(
                    [
                        jnp.where(cell_row == x * width_y + y0 + k, back, 0.0)
                        for k in range(chunk)
                    ],
                    axis=0,
                )
                surface = split_dot(spread, pick_depth, NT)
                for k in range(chunk):
                    forcing[x, y0 + k] = (
                        exc_ref[x, y0 + k] + surface[k * exc_count : (k + 1) * exc_count]
                    )

        if it == 0:
            for k, pair in enumerate(near_mat):
                def zero(k=k):
                    mat_near[k] = jnp.zeros(mat_ref.shape, jnp.int32)

                land(pair[0], pair[1], lambda: None, zero)
        rows = pl.ds(2, width_x)
        land_into(got_y[0], pe.at[rows, pl.ds(0, 2)], ay.at[it, 0])
        land_into(got_y[1], pe.at[rows, pl.ds(width_y + 2, 2)], ay.at[it, 1])
        for k, (dv, ds) in enumerate(((1, 1), (1, -1), (-1, 1), (-1, -1))):
            x = 1 if dv > 0 else width_x + 2
            y = 1 if ds > 0 else width_y + 2
            land_into(got_c[k], pe.at[x, y], ac.at[it, k])

        def land_outer(part):
            span = pl.ds(part * chunk_rows, chunk_rows)
            cols = pl.ds(2 + part * chunk_rows, chunk_rows)
            low, high = got_x[part]
            land_into(low, pe.at[pl.ds(0, 2), cols], ax.at[it, 0, :, span])
            land_into(high, pe.at[pl.ds(width_x + 2, 2), cols], ax.at[it, 1, :, span])

        def write_first(x, y, value):
            pf[x + 1, y + 1] = value
            b_send[it, x, y] = value.astype(jnp.bfloat16)

        block = b_send.at[it]
        got_b = []

        def first_sweep(part):
            sweep(part, lambda x, y: pe[x + 2, y + 2], write_first)
            span = pl.ds(part * chunk_rows, chunk_rows)
            place = base_sem + 8 + 2 * chunk_count + 2 * part
            got_b.append(
                (
                    send_near((1, 0), block.at[last_layer, span], bx.at[it, 0, :, span], place),
                    send_near(
                        (-1, 0), block.at[pl.ds(0, 1), span], bx.at[it, 1, :, span], place + 1
                    ),
                )
            )

        for part in range(chunk_count + 2):
            if part < chunk_count:
                land_outer(part)
            if 0 <= part - 1 < chunk_count:
                nu_chunk(part - 1)
            if 0 <= part - 2 < chunk_count:
                first_sweep(part - 2)
        got_y = [
            send_near(
                (0, 1), block.at[:, pl.ds(width_y - 1, 1)], by.at[it, 0], base_sem + 6
            ),
            send_near((0, -1), block.at[:, pl.ds(0, 1)], by.at[it, 1], base_sem + 7),
        ]
        if it == ITERS - 1:
            target_block = 256

            def one_block(index, carry):
                span = pl.ds(pl.multiple_of(index * target_block, target_block), target_block)
                points = jnp.concatenate(
                    [
                        as_columns(
                            points_ref[
                                :,
                                pl.ds(
                                    pl.multiple_of(index * target_block + k, LANES), LANES
                                ),
                            ]
                        )
                        for k in range(0, target_block, LANES)
                    ],
                    axis=0,
                )
                columns = [points[:, 3 + c : 4 + c] for c in range(3)]
                total = jnp.zeros((target_block, exc_count), jnp.float32)
                for k in range(0, vol_count * LANES, 2 * LANES):
                    part = slice(k, k + 2 * LANES)
                    tile = pair_kernel(columns, [ge_all[c : c + 1, part] for c in range(3)])
                    total = total + lax.dot_general(
                        tile, dens_all[:, part], NT, preferred_element_type=jnp.float32
                    )
                flux_ref[span, :] = total * flux_scale
                return carry

            lax.fori_loop(0, points_ref.shape[1] // target_block, one_block, 0)
        rows = pl.ds(1, width_x)
        land_into(got_y[0], pf.at[rows, pl.ds(0, 1)], by.at[it, 0])
        land_into(got_y[1], pf.at[rows, pl.ds(width_y + 1, 1)], by.at[it, 1])
        def write_second(x, y, value):
            if it == ITERS - 1:
                out_ref[x, y] = value
            else:
                pe[x + 2, y + 2] = value
                a_send[it + 1, x, y] = value.astype(jnp.bfloat16)

        for part in range(chunk_count):
            span = pl.ds(part * chunk_rows, chunk_rows)
            cols = pl.ds(1 + part * chunk_rows, chunk_rows)
            low, high = got_b[part]
            land_into(low, pf.at[pl.ds(0, 1), cols], bx.at[it, 0, :, span])
            land_into(high, pf.at[pl.ds(width_x + 1, 1), cols], bx.at[it, 1, :, span])
            sweep(part, lambda x, y: pf[x + 1, y + 1], write_second)

    for sends, copy in started:
        pl.when(sends)(copy.wait_send)
    others(src_count, s, lambda other: geo_pair(other, s).wait_send())
    others(vol_count, v, lambda other: geo_copy(other, v).wait_send())
    for it in range(ITERS):
        others(vol_count, v, lambda other: trace_copy(it, other, v).wait_send())
        others(src_count, s, lambda other: density_pair(it, other, s).wait_send())
        others(vol_count, v, lambda other: density_copy(it, other, v).wait_send())


def fused(
    excitation, start, material, face_cell, face_count, face_weight, slot_panel,
    target_points, source_points,
):
    vol_count, src_count = lax.axis_size("vol"), lax.axis_size("src")
    exc_count, width_x, width_y, depth = excitation.shape
    slot_count = face_cell.size
    capacity = slot_count // vol_count
    piece_len = source_points.shape[1] // vol_count
    vmem = pl.BlockSpec(memory_space=pltpu.VMEM)
    field = (width_x, width_y, exc_count, depth)
    plane = (exc_count, depth)
    f32, bf16 = jnp.float32, jnp.bfloat16
    halo_sems = ITERS * (8 + width_y) + 4
    sources = vol_count * LANES
    dma = pltpu.SemaphoreType.DMA
    potential, flux = pl.pallas_call(
        functools.partial(
            fused_kernel, vol_count, src_count, capacity, float(P_SIZE) ** (-0.5)
        ),
        out_shape=(
            jax.ShapeDtypeStruct(field, f32),
            jax.ShapeDtypeStruct((piece_len, exc_count), f32),
        ),
        in_specs=[vmem] * 9,
        out_specs=(vmem, vmem),
        scratch_shapes=[
            pltpu.VMEM((width_x + 4, width_y + 4) + plane, f32),
            pltpu.VMEM((width_x + 2, width_y + 2) + plane, f32),
            pltpu.VMEM((width_x + 2, width_y + 2) + plane, f32),
            pltpu.VMEM(field, f32),
            pltpu.VMEM((ITERS,) + field, bf16),
            pltpu.VMEM((ITERS, 2, 2, width_y) + plane, bf16),
            pltpu.VMEM((ITERS, 2, width_x, 2) + plane, bf16),
            pltpu.VMEM((ITERS, 4) + plane, bf16),
            pltpu.VMEM((ITERS,) + field, bf16),
            pltpu.VMEM((ITERS, 2, 1, width_y) + plane, bf16),
            pltpu.VMEM((ITERS, 2, width_x, 1) + plane, bf16),
            pltpu.VMEM((4, width_x, width_y, depth), jnp.int32),
            pltpu.VMEM((ITERS, LANES, LANES), f32),
            pltpu.VMEM((ITERS, vol_count, TILE, LANES), f32),
            pltpu.VMEM((ITERS, exc_count, LANES), bf16),
            pltpu.VMEM((ITERS, vol_count, exc_count, LANES), bf16),
            pltpu.VMEM((vol_count, TILE, LANES), f32),
            pltpu.VMEM((TILE, sources), f32),
            pltpu.VMEM((LANES, sources), bf16),
            pltpu.VMEM((exc_count, sources), bf16),
            pltpu.VMEM((TILE, piece_len), f32),
            pltpu.VMEM((TILE, LANES), f32),
            pltpu.VMEM((src_count, TILE, LANES), f32),
            pltpu.VMEM((TILE, LANES), f32),
            pltpu.VMEM((ITERS, exc_count, LANES), bf16),
            pltpu.VMEM((ITERS, src_count, exc_count, LANES), bf16),
            dma((src_count,)),
            dma((src_count,)),
            dma((ITERS, src_count)),
            dma((ITERS, src_count)),
            dma((halo_sems,)),
            dma((halo_sems,)),
            dma((ITERS, vol_count)),
            dma((ITERS, vol_count)),
            dma((ITERS, vol_count)),
            dma((ITERS, vol_count)),
            dma((vol_count,)),
            dma((vol_count,)),
        ],
        compiler_params=pltpu.CompilerParams(
            collective_id=0, has_side_effects=True, vmem_limit_bytes=40 * 1024 * 1024
        ),
    )(
        start.transpose(1, 2, 0, 3),
        excitation.transpose(1, 2, 0, 3),
        material,
        face_cell.reshape(1, -1),
        face_count.reshape(1, -1),
        face_weight.reshape(1, -1),
        slot_panel.reshape(1, -1),
        target_points,
        source_points,
    )
    return potential.transpose(2, 0, 1, 3), flux.T


def per_device(
    excitation,
    start,
    material,
    face_cell,
    face_count,
    face_weight,
    slot_panel,
    target_points,
    source_points,
):
    vol_count = lax.axis_size("vol")
    first_x = lax.axis_index("vol") == 0
    last_x = lax.axis_index("vol") == vol_count - 1
    first_y = lax.axis_index("src") == 0
    last_y = lax.axis_index("src") == lax.axis_size("src") - 1
    domain_edges = (first_x, last_x, first_y, last_y)
    exc_count, width_x, width_y, depth_len = excitation.shape
    cell_count = width_x * width_y * depth_len
    slot_cells = face_cell.reshape(-1)
    slot_count = slot_cells.shape[0]
    capacity = slot_count // vol_count
    piece_len = source_points.shape[1] // vol_count
    target_len = target_points.shape[1]
    lane_tile = LANES == depth_len == slot_count * lax.axis_size("src")
    if (
        lane_tile
        and vol_count * TILE == LANES
        and TILE % capacity == 0
        and LANES % exc_count == 0
        and exc_count % 16 == 0
        and width_x >= 2
        and width_y % 8 == 0
        and piece_len % 256 == 0
        and piece_len * lax.axis_size("src") == target_len
    ):
        return fused(
            excitation, start, material, face_cell, face_count, face_weight, slot_panel,
            target_points, source_points,
        )
    slot_rank = jnp.arange(slot_count, dtype=jnp.int32) % capacity
    live_count = jnp.repeat(face_count.reshape(-1), capacity, total_repeat_length=slot_count)
    slot_scale = jnp.where(slot_rank < live_count, face_weight.reshape(-1), 0.0)
    compact = slot_count < piece_len
    vol_index = lax.axis_index("vol")
    src_index = lax.axis_index("src")
    src_count = lax.axis_size("src")
    panels = slot_panel.reshape(-1)
    if compact:
        own_points = jnp.concatenate(
            [
                jnp.take(lax.dynamic_slice_in_dim(source_points, vol_index * piece_len, piece_len, 1), panels, axis=1),
                jnp.take(lax.dynamic_slice_in_dim(target_points, src_index * piece_len, piece_len, 1), panels, axis=1),
                panels.astype(jnp.float32)[None],
            ]
        )
        own_targets = lax.dynamic_slice_in_dim(target_points, src_index * piece_len, piece_len, 1)
    else:
        owner_table = (
            panels[:, None] == jnp.arange(piece_len, dtype=jnp.int32)[None, :]
        ).astype(jnp.float32)
    flux_scale = float(P_SIZE) ** (-0.5)
    potential = start
    flux_own = jnp.zeros((exc_count, piece_len), jnp.float32)
    for outer_index in range(ITERS):
        current = with_rim(potential)
        nu_own = reluctivity(gradient_sq(pad_depth(current)), material)
        nu_ext = extended(nu_own, (("vol", 1), ("src", 2)), 1)
        weights = face_weights(nu_ext, domain_edges)
        diagonal = weights[0] + weights[1] + weights[2] + weights[3] + weights[4] + weights[5]
        cell_values = jnp.take(potential.reshape(exc_count, cell_count), slot_cells, axis=1)
        if compact:
            traces = (cell_values * slot_scale[None, :]).T
            message = traces if outer_index else jnp.concatenate([traces, own_points.T], axis=1)
            gathered = lax.all_gather(message, ("vol", "src"), axis=0, tiled=False)
            gathered = gathered.reshape(vol_count, src_count, slot_count, -1)
            if outer_index == 0:
                points = gathered[..., exc_count:]
                places = points[..., :3].reshape(-1, 3).T
                ids = points[..., 6]
                same = ids[..., :, None] == ids[..., None, :]
                rank = jnp.arange(slot_count)
                earlier = same & (rank[None, :] < rank[:, None])
                merge = (same & ~jnp.any(earlier, axis=-1)[..., None]).astype(jnp.float32)
                mine = lax.dynamic_index_in_dim(points, src_index, 1, keepdims=False)
                mine = mine.reshape(vol_count, vol_count, capacity, -1)
                mine = lax.dynamic_index_in_dim(mine, vol_index, 1, keepdims=False)
                slot_targets = mine[..., 3:6].reshape(-1, 3).T
                slot_kernel = kernel_block(slot_targets, places)
            arrived = gathered[..., :exc_count].reshape(
                vol_count, src_count, vol_count, capacity, exc_count
            )
            arrived = arrived.transpose(2, 1, 0, 3, 4).reshape(
                vol_count, src_count, slot_count, exc_count
            )
            density = jnp.einsum(
                "wsij,wsje->wsie", merge, arrived, precision=lax.Precision.HIGHEST
            )
            density = density.reshape(-1, exc_count).astype(jnp.bfloat16)
            returned = flux_scale * jnp.einsum(
                "tn,ne->te", slot_kernel, density, preferred_element_type=jnp.float32
            )
            if outer_index == ITERS - 1:
                flux_own = flux_scale * jnp.einsum(
                    "ne,tn->et",
                    density,
                    kernel_block(own_targets, places),
                    preferred_element_type=jnp.float32,
                )
        else:
            outgoing = (cell_values * slot_scale[None, :]).T.reshape(vol_count, capacity * exc_count)
            arrived = lax.all_to_all(outgoing, "vol", split_axis=0, concat_axis=0, tiled=True).reshape(
                slot_count, exc_count
            )
            density = jnp.dot(
                arrived.T,
                owner_table,
                precision=lax.Precision.HIGHEST,
                preferred_element_type=jnp.float32,
            ).astype(jnp.bfloat16)
            block_piece = lax.all_gather(density, "vol", axis=1, tiled=True)
            piece_count = block_piece.shape[1]
            step_len = 1024

            def one_step(step_index, partial_value):
                offset_index = step_index * step_len
                segment = lax.dynamic_slice_in_dim(block_piece, offset_index, step_len, 1)
                places = lax.dynamic_slice_in_dim(source_points, offset_index, step_len, 1)
                dist_sq = jnp.zeros((target_len, step_len), jnp.float32)
                for component in range(3):
                    offset = target_points[component][:, None] - places[component][None, :]
                    dist_sq = dist_sq + offset * offset
                kernel = lax.rsqrt(dist_sq + SOFTENING * SOFTENING).astype(jnp.bfloat16)
                return partial_value + jnp.einsum(
                    "en,tn->et", segment, kernel, preferred_element_type=jnp.float32
                )

            partial_flux = lax.fori_loop(
                0, piece_count // step_len, one_step, jnp.zeros((exc_count, target_len), jnp.float32)
            )
            flux_sum = lax.psum_scatter(partial_flux, "src", scatter_dimension=1, tiled=True)
            flux_own = flux_sum * flux_scale
            per_slot = jnp.dot(
                flux_own,
                owner_table.T,
                precision=lax.Precision.HIGHEST,
                preferred_element_type=jnp.float32,
            )
            returned = lax.all_to_all(
                per_slot.T.reshape(vol_count, capacity * exc_count),
                "vol",
                split_axis=0,
                concat_axis=0,
                tiled=True,
            ).reshape(slot_count, exc_count)
        contribution = returned.T * slot_scale[None, :]
        surface = (
            jnp.zeros((exc_count, cell_count), jnp.float32).at[:, slot_cells].add(contribution)
        )
        forcing = excitation + surface.reshape(excitation.shape)
        for sweep_index in range(SWEEPS):
            if sweep_index > 0:
                current = with_rim(potential)
            potential = relax(pad_depth(current), weights, diagonal, forcing)
    return (potential, flux_own)


def solution(mesh):
    return jax.shard_map(
        per_device,
        mesh=mesh,
        in_specs=(
            P(None, "vol", "src", None),
            P(None, "vol", "src", None),
            P("vol", "src", None),
            P("vol", "src", None),
            P("vol", "src", None),
            P("vol", "src", None),
            P("vol", "src", None),
            P(None, "vol"),
            P(None, "src"),
        ),
        out_specs=(P(None, "vol", "src", None), P(None, ("vol", "src"))),
        check_vma=False,
    )
```
